256 devices in a mesh: segment: 4 (over y_lo, core), tile: 64 (over x, y_hi, z).
Axes of the slice: x: 4, y: 4 (y_hi: 2, y_lo: 2; y = y_hi * 2 + y_lo), z: 8, core: 2. Of those that a mesh axis runs over, the one named last changes fastest.
Arguments:
- slide_pixels: bfloat16 [128, 4096, 208], P('segment', 'tile'), may hold values from -6 to 6
- taps_fine: float32 [3, 3, 208], replicated, may hold values from -2 to 2
- mix_fine: bfloat16 [208, 208], replicated, may hold values from -0.4375 to 0.4375
- reduce_weight: bfloat16 [832, 416], replicated, may hold values from -0.21875 to 0.21875
- taps_coarse: float32 [5, 5, 416], replicated, may hold values from -1.25 to 1.25
- mix_coarse: bfloat16 [416, 416], replicated, may hold values from -0.3125 to 0.3125
- cotangent: bfloat16 [64, 2048, 416], P('segment', 'tile'), may hold values from -6 to 6
Outputs:
- section_out: bfloat16 [64, 2048, 416], P('segment', 'tile')
- pixel_grad: bfloat16 [128, 4096, 208], P('segment', 'tile')
- grad_taps_fine: float32 [3, 3, 208], replicated
- grad_mix_fine: float32 [208, 208], replicated
- grad_reduce: float32 [832, 416], replicated
- grad_taps_coarse: float32 [5, 5, 416], replicated
- grad_mix_coarse: float32 [416, 416], replicated
The draws below stay inside these ranges and needn't reach their ends.
All inputs are finite; a program needn't handle non-finite values.
Results may differ from the reference program's by a relative error of at most 0.022.
Values may be sent and summed in bfloat16 or wider, within the bound.
No kernel may reach another device: no remote copies, remote signals or barrier semaphores. Data moves between devices by JAX's collectives and lax.ppermute only.
A program may use at most 64 MiB of HBM per device.

```python
import jax
import jax.numpy as jnp
from jax import lax

C1 = 208
C2 = 416
NR = 128
NC = 4096


def shard_levels(key, shape, pieces, low, high):
    factor_of, own = 1.0, jax.random.fold_in(key, 6)
    for position, parts in pieces:
        heights = jnp.exp(jax.random.uniform(jax.random.fold_in(own, position), (parts,), jnp.float32, low / len(pieces), high / len(pieces)))
        factor_of = factor_of * jnp.repeat(heights, shape[position] // parts).reshape([-1 if axis == position else 1 for axis in range(len(shape))])
    return factor_of


def gaussian(rng, shape, width, limit, split=(), kind=jnp.bfloat16):
    gain = shard_levels(rng, shape, split, -0.22, 0.18) if split else 1.0
    values = jax.random.normal(rng, shape, jnp.float32) * width * gain
    return jnp.minimum(jnp.maximum(values, -limit), limit).astype(kind)


def setup_inputs(seed: int = 0) -> dict:
    splits = jax.random.split(jax.random.key(seed), 8)
    slide_pixels = gaussian(splits[0], (NR, NC, C1), 1.0, 6.0, ((0, 4), (1, 64)))
    taps_fine = gaussian(splits[1], (3, 3, C1), 0.33, 2.0, (), jnp.float32)
    mix_fine = gaussian(splits[2], (C1, C1), C1 ** -0.5, 0.4375)
    reduce_weight = gaussian(splits[3], (4 * C1, C2), (4 * C1) ** -0.5, 0.21875)
    taps_coarse = gaussian(splits[4], (5, 5, C2), 0.2, 1.25, (), jnp.float32)
    mix_coarse = gaussian(splits[5], (C2, C2), C2 ** -0.5, 0.3125)
    cotangent = gaussian(splits[6], (NR // 2, NC // 2, C2), 1.0, 6.0, ((0, 4), (1, 64)))
    return dict(slide_pixels=slide_pixels, taps_fine=taps_fine, mix_fine=mix_fine, reduce_weight=reduce_weight, taps_coarse=taps_coarse, mix_coarse=mix_coarse, cotangent=cotangent)


def depthwise(padded, taps, stride, height, breadth):
    kernel_size = taps.shape[0]
    accumulated = jnp.zeros((height, breadth, taps.shape[2]), jnp.float32)
    for row_tap in range(kernel_size):
        for col_tap in range(kernel_size):
            window = padded[row_tap * stride:row_tap * stride + height, col_tap * stride:col_tap * stride + breadth]
            accumulated = accumulated + taps[row_tap, col_tap] * window.astype(jnp.float32)
    return accumulated


def transposed(padded, taps, stride, margin, height, breadth):
    kernel_size = taps.shape[0]
    accumulated = jnp.zeros((height, breadth, taps.shape[2]), jnp.float32)
    for row_tap in range(kernel_size):
        for col_tap in range(kernel_size):
            row_start = 2 * margin - row_tap * stride
            col_start = 2 * margin - col_tap * stride
            window = padded[row_start:row_start + height, col_start:col_start + breadth]
            accumulated = accumulated + taps[row_tap, col_tap] * window.astype(jnp.float32)
    return accumulated


def tap_grads(gradient, padded, kernel_size, stride):
    height, breadth = gradient.shape[0], gradient.shape[1]
    gradient_wide = gradient.astype(jnp.float32)
    outer = []
    for row_tap in range(kernel_size):
        inner = []
        for col_tap in range(kernel_size):
            window = padded[row_tap * stride:row_tap * stride + height, col_tap * stride:col_tap * stride + breadth]
            inner.append(jnp.sum(gradient_wide * window.astype(jnp.float32), axis=(0, 1)))
        outer.append(jnp.stack(inner))
    return jnp.stack(outer)


def unshuffle(field):
    height, breadth, chans = field.shape
    return field.reshape(height // 2, 2, breadth // 2, 2, chans).transpose(0, 2, 1, 3, 4).reshape(height // 2, breadth // 2, 4 * chans)


def reshuffle(field):
    height, breadth, wide = field.shape
    chans = wide // 4
    return field.reshape(height, breadth, 2, 2, chans).transpose(0, 2, 1, 3, 4).reshape(2 * height, 2 * breadth, chans)


def pixel_product(left, right):
    return lax.dot_general(left, right, (((0, 1), (0, 1)), ((), ())), preferred_element_type=jnp.float32)


def silu_slope(field):
    value = field.astype(jnp.float32)
    sigmoid = jax.nn.sigmoid(value)
    return sigmoid * (1.0 + value * (1.0 - sigmoid))


def reference(slide_pixels, taps_fine, mix_fine, reduce_weight, taps_coarse, mix_coarse, cotangent):
    zero_bf = jnp.zeros((), jnp.bfloat16)
    relu_fine = jnp.maximum(slide_pixels, zero_bf)
    padded_fine = jnp.pad(relu_fine, ((1, 1), (1, 1), (0, 0)))
    depth_fine = depthwise(padded_fine, taps_fine, 1, NR, NC).astype(jnp.bfloat16)
    section_fine = (slide_pixels.astype(jnp.float32) + jnp.dot(depth_fine, mix_fine, preferred_element_type=jnp.float32)).astype(jnp.bfloat16)
    pre_fine = unshuffle(section_fine)
    unshuffled = jax.nn.silu(pre_fine.astype(jnp.float32)).astype(jnp.bfloat16)
    reduced = jnp.dot(unshuffled, reduce_weight, preferred_element_type=jnp.float32).astype(jnp.bfloat16)
    act_coarse = jax.nn.silu(reduced.astype(jnp.float32)).astype(jnp.bfloat16)
    padded_coarse = jnp.pad(act_coarse, ((4, 4), (4, 4), (0, 0)))
    depth_coarse = depthwise(padded_coarse, taps_coarse, 2, NR // 2, NC // 2).astype(jnp.bfloat16)
    section_out = (reduced.astype(jnp.float32) + jnp.dot(depth_coarse, mix_coarse, preferred_element_type=jnp.float32)).astype(jnp.bfloat16)

    scale_fine = float(NR * NC) ** -0.5
    scale_coarse = float(NR * NC // 4) ** -0.5
    grad_mix_coarse = pixel_product(depth_coarse, cotangent) * scale_coarse
    delta_coarse = jnp.dot(cotangent, mix_coarse.T, preferred_element_type=jnp.float32).astype(jnp.bfloat16)
    grad_taps_coarse = tap_grads(delta_coarse, padded_coarse, 5, 2) * scale_coarse
    padded_delta = jnp.pad(delta_coarse, ((4, 4), (4, 4), (0, 0)))
    back_coarse = transposed(padded_delta, taps_coarse, 2, 4, NR // 2, NC // 2).astype(jnp.bfloat16)
    delta_reduced = (cotangent.astype(jnp.float32) + back_coarse.astype(jnp.float32) * silu_slope(reduced)).astype(jnp.bfloat16)
    grad_reduce = pixel_product(unshuffled, delta_reduced) * scale_coarse
    spread = jnp.dot(delta_reduced, reduce_weight.T, preferred_element_type=jnp.float32)
    delta_fine = reshuffle(spread * silu_slope(pre_fine)).astype(jnp.bfloat16)
    grad_mix_fine = pixel_product(depth_fine, delta_fine) * scale_fine
    delta_depth = jnp.dot(delta_fine, mix_fine.T, preferred_element_type=jnp.float32).astype(jnp.bfloat16)
    grad_taps_fine = tap_grads(delta_depth, padded_fine, 3, 1) * scale_fine
    padded_back = jnp.pad(delta_depth, ((1, 1), (1, 1), (0, 0)))
    back_fine = transposed(padded_back, taps_fine, 1, 1, NR, NC)
    pixel_grad = (delta_fine.astype(jnp.float32) + jnp.where(slide_pixels > 0, back_fine, 0.0)).astype(jnp.bfloat16)
    return (section_out, pixel_grad, grad_taps_fine, grad_mix_fine, grad_reduce, grad_taps_coarse, grad_mix_coarse)
```

```python
import functools

import jax
import jax.numpy as jnp
from jax import lax
from jax.experimental import pallas as pl
from jax.experimental.pallas import tpu as pltpu
from jax.sharding import Mesh, PartitionSpec as P

ROWS = ("yl", "core")
COLS = ("x", "yh", "z")
PLANE = ("yl", "x", "yh")
BF = jnp.bfloat16
F4 = jnp.float32
LIMIT = 56 * 1024 * 1024
RED, MIXC, MIXF, TAPC, TAPF, TOTAL = 0, 832, 1248, 1456, 1488, 1536
SOURCE = ((2, 0, 1), (0, 1, 3))


def dot(left, right):
    return jnp.dot(left, right, preferred_element_type=F4)


def dot_nt(left, right):
    return lax.dot_general(left, right, (((1,), (1,)), ((), ())), preferred_element_type=F4)


def dot_tn(left, right):
    return lax.dot_general(left, right, (((0,), (0,)), ((), ())), preferred_element_type=F4)


def picker(rows, columns, source):
    row = lax.broadcasted_iota(jnp.int32, (rows, columns), 0)
    column = lax.broadcasted_iota(jnp.int32, (rows, columns), 1)
    return jnp.where(column == source(row), 1.0, 0.0).astype(BF)


def fine_source(row):
    kind, m = row // 32, row % 32
    even, odd = 2 * m, 2 * m + 1
    before = jnp.where(m == 0, 64, 2 * m - 1)
    after = jnp.where(m == 31, 65, 2 * m + 2)
    return jnp.where(kind == 0, even, jnp.where(kind == 1, odd, jnp.where(kind == 2, before, after)))


def phase_source(row):
    kind, m = row // 32, row % 32
    before = jnp.where(m == 0, 64, 32 + m - 1)
    after = jnp.where(m == 31, 65, m + 1)
    return jnp.where(kind == 0, before, after)


def weave_source(row):
    return jnp.where(row % 2 == 0, row // 2, 32 + row // 2)


def coarse_source(row):
    shift, m = row // 32, row % 32
    at = m + 2 * shift - 4
    return jnp.where(at < 0, 36 + at, jnp.where(at > 31, 4 + at, at))


def sigmoid(value):
    return 1.0 / (1.0 + jnp.exp(-value))


def fine_rows(slide_ref, top_ref, bottom_ref, lr_ref, shifted, keep=None):
    pick = picker(128, 80, fine_source)

    def put(r, row):
        got = dot(pick, jnp.concatenate([row, lr_ref[r]], axis=0))
        shifted[:, r] = jnp.maximum(got, 0.0).reshape(4, 32, got.shape[1])
        return got

    put(0, top_ref[0])
    put(33, bottom_ref[0])

    def step(i, carry):
        for p in range(2):
            got = put(2 * i + p + 1, slide_ref[2 * i + p])
            if keep is not None:
                keep[2 * p, i] = got[:32].astype(BF)
                keep[2 * p + 1, i] = got[32:64].astype(BF)
        return carry

    lax.fori_loop(0, 16, step, 0)


def fine_conv(i, shifted, taps_ref, flip, put):
    for p in range(2):
        for q in range(2):
            total = None
            for a in range(3):
                for b in range(3):
                    u, v = (2 - a, 2 - b) if flip else (a, b)
                    term = taps_ref[u, v : v + 1, :] * shifted[SOURCE[q][b], 2 * i + p + a]
                    total = term if total is None else total + term
            put(2 * p + q, total)


def fine_forward(
    slide_ref, top_ref, bottom_ref, lr_ref, taps_ref, mix_ref, weight_ref,
    slide_out, depth_out, pre_out, reduced_out, act_out, shifted, total,
):
    fine_rows(slide_ref, top_ref, bottom_ref, lr_ref, shifted, slide_out)

    def conv(i, carry):
        def put(k, value):
            depth_out[k, i] = value.astype(BF)

        fine_conv(i, shifted, taps_ref, False, put)
        return carry

    lax.fori_loop(0, 16, conv, 0)
    chans = mix_ref.shape[0]
    wide = weight_ref.shape[1]
    for k in range(4):
        mixed = dot(depth_out[k].reshape(512, chans), mix_ref[...])
        pre = (slide_out[k].reshape(512, chans).astype(F4) + mixed).astype(BF)
        pre_out[k] = pre
        value = pre.astype(F4)
        unshuffled = (value * sigmoid(value)).astype(BF)
        part = dot(unshuffled, weight_ref[k * chans : (k + 1) * chans, :])
        if k == 0:
            total[...] = part
        else:
            total[...] += part
    reduced = total[...].astype(BF)
    reduced_out[...] = reduced
    value = reduced.astype(F4)
    act_out[...] = (value * sigmoid(value)).astype(BF).reshape(16, 32, wide)


def coarse_rows(row_of, lr_of, shifted):
    pick = picker(160, 48, coarse_source)

    def step(r, carry):
        got = dot(pick, jnp.concatenate([row_of(r), lr_of(r)], axis=0))
        shifted[:, r] = got.reshape(5, 32, got.shape[1])
        return carry

    lax.fori_loop(0, 24, step, 0)


def backward(
    cot_ref, tb_ref, lr_ref, mixc_ref, tapsc_ref, reduced_ref, pre_ref, depth_ref, weight_ref, mix_ref,
    slide_ref, top_ref, bottom_ref, lrf_ref,
    deltac_out, dfine_out, ddepth_out, gred_out, gmix_out, gtaps_out,
    delta, delta_lr, shiftc, delta_red, shifted,
):
    wide = mixc_ref.shape[0]
    chans = mix_ref.shape[0]
    mixc = mixc_ref[...]
    inner = dot_nt(cot_ref[...].reshape(512, wide), mixc).astype(BF).reshape(16, 32, wide)
    delta[4:20] = inner
    deltac_out[...] = inner
    edge = dot_nt(tb_ref[...].reshape(256, wide), mixc).astype(BF).reshape(8, 32, wide)
    delta[0:4] = edge[:4]
    delta[20:24] = edge[4:]
    delta_lr[...] = dot_nt(lr_ref[...].reshape(384, wide), mixc).astype(BF).reshape(24, 16, wide)
    coarse_rows(lambda r: delta[r], lambda r: delta_lr[r], shiftc)

    def conv(i, carry):
        total = None
        for a in range(5):
            for b in range(5):
                term = tapsc_ref[4 - a, 4 - b : 5 - b, :] * shiftc[b, i + 2 * a]
                total = term if total is None else total + term
        back = total.astype(BF).astype(F4)
        value = reduced_ref[i].astype(F4)
        s = sigmoid(value)
        slope = s * (1.0 + value * (1.0 - s))
        delta_red[i] = (cot_ref[i].astype(F4) + back * slope).astype(BF)
        return carry

    lax.fori_loop(0, 16, conv, 0)
    fine_rows(slide_ref, top_ref, bottom_ref, lrf_ref, shifted)
    red = delta_red[...].reshape(512, wide)
    for k in range(4):
        value = pre_ref[k].astype(F4)
        s = sigmoid(value)
        unshuffled = (value * s).astype(BF)
        gred_out[k * chans : (k + 1) * chans, :] = dot_tn(unshuffled, red).astype(BF)
        spread = dot_nt(red, weight_ref[k * chans : (k + 1) * chans, :])
        dfine = (spread * (s * (1.0 + value * (1.0 - s)))).astype(BF)
        dfine_out[k] = dfine.reshape(16, 32, chans)
        part = dot_tn(depth_ref[k], dfine)
        if k == 0:
            gmix_out[...] = part
        else:
            gmix_out[...] += part
        ddepth_out[k] = dot_nt(dfine, mix_ref[...]).astype(BF).reshape(16, 32, chans)

    def taps(i, sums):
        for p in range(2):
            for q in range(2):
                grad = ddepth_out[2 * p + q, i].astype(F4)
                fresh = []
                for a in range(3):
                    for b in range(3):
                        term = grad * shifted[SOURCE[q][b], 2 * i + p + a]
                        fresh.append(sums[3 * a + b] + jnp.sum(term.reshape(4, 8, chans), axis=0))
                sums = tuple(fresh)
        return sums

    sums = lax.fori_loop(0, 16, taps, tuple(jnp.zeros((8, chans), F4) for _ in range(9)))
    gtaps_out[...] = jnp.zeros_like(gtaps_out)
    for at in range(9):
        gtaps_out[at : at + 1, :] = jnp.sum(sums[at], axis=0, keepdims=True)


def coarse_forward(
    act_ref, top_ref, bottom_ref, lr_ref, taps_ref, mix_ref, reduced_ref, cot_ref, deltac_ref,
    gred_ref, gmixf_ref, gtapsf_ref, core_ref,
    section_out, mine_out, other_out, shifted, sums, depth, rows, packed,
):
    wide = mix_ref.shape[0]
    rows[0:4] = top_ref[...]
    rows[4:20] = act_ref[...]
    rows[20:24] = bottom_ref[...]
    coarse_rows(lambda r: rows[r], lambda r: lr_ref[r], shifted)
    sums[...] = jnp.zeros_like(sums)

    def conv(i, carry):
        total = None
        grad = deltac_ref[i].astype(F4)
        for a in range(5):
            for b in range(5):
                at = 5 * a + b
                window = shifted[b, i + 2 * a]
                term = taps_ref[a, b : b + 1, :] * window
                total = term if total is None else total + term
                sums[at] += jnp.sum((grad * window).reshape(4, 8, wide), axis=0)
        depth[i] = total.astype(BF)
        return carry

    lax.fori_loop(0, 16, conv, 0)
    flat = depth[...].reshape(512, wide)
    section_out[...] = (reduced_ref[...].reshape(512, wide).astype(F4) + dot(flat, mix_ref[...])).astype(BF).reshape(16, 32, wide)
    fine = gmixf_ref.shape[0]
    packed[RED:MIXC, :] = gred_ref[...]
    packed[MIXC:MIXF, :] = dot_tn(flat, cot_ref[...].reshape(512, wide)).astype(BF)
    packed[MIXF:, :] = jnp.zeros((TOTAL - MIXF, wide), BF)
    packed[MIXF:TAPC, 0:fine] = gmixf_ref[...].astype(BF)
    taps = jnp.concatenate([jnp.sum(sums[...], axis=1), jnp.zeros((7, wide), F4)], axis=0)
    packed[TAPC:TAPF, :] = taps.astype(BF)
    packed[TAPF : TAPF + 16, 0:fine] = gtapsf_ref[...].astype(BF)
    core = core_ref[0]
    half = TOTAL // 2
    mine_out[...] = packed[pl.ds(pl.multiple_of(core * half, half), half), :]
    other_out[...] = packed[pl.ds(pl.multiple_of((1 - core) * half, half), half), :]


def unpack(
    near_ref, far_ref, core_ref, tapsf_out, mixf_out, red_out, tapsc_out, mixc_out, packed, *, fine, coarse
):
    core = core_ref[0]
    half = TOTAL // 2
    packed[pl.ds(pl.multiple_of(core * half, half), half), :] = near_ref[...]
    packed[pl.ds(pl.multiple_of((1 - core) * half, half), half), :] = far_ref[...]
    chans = mixf_out.shape[0]
    red_out[...] = packed[RED:MIXC, :].astype(F4) * coarse
    mixc_out[...] = packed[MIXC:MIXF, :].astype(F4) * coarse
    mixf_out[...] = packed[MIXF:TAPC, 0:chans].astype(F4) * fine
    taps = packed[TAPC:TAPF, :].astype(F4) * coarse
    for a in range(5):
        tapsc_out[a] = taps[5 * a : 5 * a + 5]
    taps = packed[TAPF : TAPF + 16, 0:chans].astype(F4) * fine
    for a in range(3):
        tapsf_out[a] = taps[3 * a : 3 * a + 3]


def fine_backward(
    ddepth_ref, top_ref, bottom_ref, lr_ref, taps_ref, dfine_ref, slide_ref, out_ref, shifted
):
    chans = taps_ref.shape[2]
    pick = picker(64, 80, phase_source)
    weave = picker(64, 64, weave_source)

    def put(r, even, odd):
        got = dot(pick, jnp.concatenate([even, odd, lr_ref[r]], axis=0))
        shifted[0, r] = even.astype(F4)
        shifted[1, r] = odd.astype(F4)
        shifted[2, r] = got[:32]
        shifted[3, r] = got[32:]

    put(0, top_ref[0], top_ref[1])
    put(33, bottom_ref[0], bottom_ref[1])

    def fill(i, carry):
        for p in range(2):
            put(2 * i + p + 1, ddepth_ref[2 * p, i], ddepth_ref[2 * p + 1, i])
        return carry

    lax.fori_loop(0, 16, fill, 0)

    def conv(i, carry):
        found = {}

        def put_one(k, value):
            slide = slide_ref[k, i].astype(F4)
            kept = jnp.where(slide > 0, value, 0.0)
            found[k] = (dfine_ref[k, i].astype(F4) + kept).astype(BF)

        fine_conv(i, shifted, taps_ref, True, put_one)
        for p in range(2):
            both = jnp.concatenate([found[2 * p], found[2 * p + 1]], axis=0)
            out_ref[2 * i + p] = dot(weave, both).astype(BF)
        return carry

    lax.fori_loop(0, 16, conv, 0)


def call(body, outs, scratch, flops, *operands):
    def spec(kind):
        return pl.BlockSpec(memory_space=pltpu.SMEM if kind == jnp.int32 else pltpu.VMEM)

    return pl.pallas_call(
        body,
        out_shape=[jax.ShapeDtypeStruct(shape, kind) for shape, kind in outs],
        in_specs=[spec(operand.dtype) for operand in operands],
        out_specs=[spec(kind) for _, kind in outs],
        scratch_shapes=[pltpu.VMEM(shape, kind) for shape, kind in scratch],
        compiler_params=pltpu.CompilerParams(vmem_limit_bytes=LIMIT),
        cost_estimate=pl.CostEstimate(flops=flops, bytes_accessed=8_000_000, transcendentals=0),
    )(*operands)


def swap(first, last, axes):
    count = lax.axis_size(axes)
    even = lax.axis_index(axes) % 2 == 0
    near = lax.ppermute(jnp.where(even, last, first), axes, [(i, i ^ 1) for i in range(count)])
    far = [(i, i + 1) for i in range(1, count - 1, 2)]
    far = far + [(j, i) for i, j in far]
    away = lax.ppermute(jnp.where(even, first, last), axes, far)
    return jnp.where(even, away, near), jnp.where(even, near, away)


def halos(coarse, fine_top, fine_bottom, fine_left, fine_right):
    height, breadth, wide = coarse.shape
    chans = fine_top.shape[-1]

    def widen(rows):
        return jnp.pad(rows, ((0, 0), (0, wide - chans)))

    first = jnp.concatenate([coarse[:4].reshape(4 * breadth, wide), widen(fine_top)], axis=0)
    last = jnp.concatenate([coarse[-4:].reshape(4 * breadth, wide), widen(fine_bottom)], axis=0)
    low, high = swap(first, last, ROWS)
    split = 4 * breadth
    top, bottom = low[:split].reshape(4, breadth, wide), high[:split].reshape(4, breadth, wide)
    fine_low, fine_high = low[split:, :chans], high[split:, :chans]

    def column(at, edge, pixels):
        parts = [
            jnp.concatenate([top[:, at + s], coarse[:, at + s], bottom[:, at + s]], axis=0)
            for s in range(4)
        ]
        ends = [fine_low[edge : edge + 1], pixels, fine_high[edge : edge + 1]]
        return jnp.concatenate(parts + [widen(jnp.concatenate(ends, axis=0))], axis=0)

    left, right = swap(
        column(0, 0, fine_left),
        column(breadth - 4, fine_low.shape[0] - 1, fine_right),
        COLS,
    )
    tall = height + 8

    def spread(block):
        return block[: 4 * tall].reshape(4, tall, wide).transpose(1, 0, 2)

    sides_coarse = sides(spread(left), spread(right))
    sides_fine = sides(left[4 * tall :, None, :chans], right[4 * tall :, None, :chans])
    return top, bottom, sides_coarse, fine_low, fine_high, sides_fine


def reduce_terms(mine, other):
    total, wide = mine.shape
    core = lax.axis_index("core")
    plane = lax.axis_size(PLANE)
    depth = lax.axis_size("z")
    trade = [(0, 1), (1, 0)]
    mine = mine.astype(F4) + lax.ppermute(other, "core", trade).astype(F4)
    chunk = total // plane
    got = lax.all_to_all(mine.astype(BF).reshape(plane, chunk, wide), PLANE, 0, 0, tiled=True)
    mine = jnp.sum(got.astype(F4), axis=0).astype(BF)
    got = lax.all_to_all(jnp.broadcast_to(mine, (depth, chunk, wide)), "z", 0, 0, tiled=True)
    mine = jnp.sum(got.astype(F4), axis=0).astype(BF)
    got = lax.all_to_all(jnp.broadcast_to(mine, (plane, chunk, wide)), PLANE, 0, 0, tiled=True)
    got = got.reshape(total, wide)
    return got, lax.ppermute(got, "core", trade)


def sides(left, right):
    both = jnp.concatenate([left, right], axis=1)
    return jnp.pad(both, ((0, 0), (0, 16 - both.shape[1]), (0, 0)))


def shards(slide_pixels, taps_fine, mix_fine, reduce_weight, taps_coarse, mix_coarse, cotangent):
    height, breadth, chans = slide_pixels.shape
    wide = cotangent.shape[2]
    devices_all = lax.axis_size(ROWS) * lax.axis_size(COLS)
    scale_fine = float(height * breadth * devices_all) ** (-0.5)
    scale_coarse = float(height * breadth // 4 * devices_all) ** (-0.5)
    core = lax.axis_index("core").astype(jnp.int32).reshape(1)
    ctop, cbottom, clr, top, bottom, lr = halos(
        cotangent, slide_pixels[0], slide_pixels[-1], slide_pixels[:, 0], slide_pixels[:, -1]
    )
    top, bottom = top[None], bottom[None]

    slide, depth, pre, reduced, act = call(
        fine_forward,
        [
            ((4, 16, 32, chans), BF),
            ((4, 16, 32, chans), BF),
            ((4, 512, chans), BF),
            ((512, wide), BF),
            ((16, 32, wide), BF),
        ],
        [((4, 34, 32, chans), F4), ((512, wide), F4)],
        4_000_000_000,
        slide_pixels, top, bottom, lr, taps_fine, mix_fine, reduce_weight,
    )
    reduced = reduced.reshape(16, 32, wide)

    delta_coarse, dfine, ddepth, term_reduce, term_mix_fine, term_taps_fine = call(
        backward,
        [
            ((16, 32, wide), BF),
            ((4, 16, 32, chans), BF),
            ((4, 16, 32, chans), BF),
            ((4 * chans, wide), BF),
            ((chans, chans), F4),
            ((16, chans), F4),
        ],
        [
            ((24, 32, wide), BF),
            ((24, 16, wide), BF),
            ((5, 24, 32, wide), F4),
            ((16, 32, wide), BF),
            ((4, 34, 32, chans), F4),
        ],
        8_000_000_000,
        cotangent, jnp.concatenate([ctop, cbottom], axis=0), clr, mix_coarse, taps_coarse, reduced, pre,
        depth.reshape(4, 512, chans), reduce_weight, mix_fine, slide_pixels, top, bottom, lr,
    )

    inner = ddepth.reshape(2, 2, 16, 32, chans)
    atop, abottom, alr, dtop, dbottom, dlr = halos(
        act,
        ddepth[:2, 0].reshape(breadth, chans),
        ddepth[2:, 15].reshape(breadth, chans),
        inner[:, 0, :, 0].transpose(1, 0, 2).reshape(height, chans),
        inner[:, 1, :, 31].transpose(1, 0, 2).reshape(height, chans),
    )
    section_out, mine, other = call(
        coarse_forward,
        [((16, 32, wide), BF), ((TOTAL // 2, wide), BF), ((TOTAL // 2, wide), BF)],
        [
            ((5, 24, 32, wide), F4),
            ((25, 8, wide), F4),
            ((16, 32, wide), BF),
            ((24, 32, wide), BF),
            ((TOTAL, wide), BF),
        ],
        4_000_000_000,
        act, atop, abottom, alr, taps_coarse, mix_coarse, reduced, cotangent, delta_coarse,
        term_reduce, term_mix_fine, term_taps_fine, core,
    )
    (pixel_grad,) = call(
        fine_backward,
        [((height, breadth, chans), BF)],
        [((4, 34, 32, chans), F4)],
        2_000_000_000,
        ddepth, dtop.reshape(2, 32, chans), dbottom.reshape(2, 32, chans), dlr, taps_fine, dfine, slide,
    )
    near, far = reduce_terms(mine, other)
    grads = call(
        functools.partial(unpack, fine=scale_fine, coarse=scale_coarse),
        [
            ((3, 3, chans), F4),
            ((chans, chans), F4),
            ((4 * chans, wide), F4),
            ((5, 5, wide), F4),
            ((wide, wide), F4),
        ],
        [((TOTAL, wide), BF)],
        1_000_000,
        near, far, core,
    )
    return (section_out, pixel_grad, *grads)


def solution(mesh):
    fine = Mesh(mesh.devices.reshape(2, 2, 4, 2, 8), ("yl", "core", "x", "yh", "z"))
    tiles = P(ROWS, COLS, None)
    return jax.shard_map(
        shards,
        mesh=fine,
        in_specs=(tiles, P(), P(), P(), P(), P(), tiles),
        out_specs=(tiles, tiles, P(), P(), P(), P(), P()),
        check_vma=False,
    )
```

```python
import functools

import jax
import jax.numpy as jnp
from jax import lax
from jax.experimental import pallas as pl
from jax.experimental.pallas import tpu as pltpu
from jax.sharding import Mesh, PartitionSpec as P

ROWS = ("yl", "core")
COLS = ("x", "yh", "z")
PLANE = ("yl", "x", "yh")
BF = jnp.bfloat16
F4 = jnp.float32
LIMIT = 56 * 1024 * 1024
RED, MIXC, MIXF, TAPC, TAPF, TOTAL = 0, 832, 1248, 1456, 1488, 1536
LANES = 512
SOURCE = ((2, 0, 1), (0, 1, 3))


def dot(left, right):
    return jnp.dot(left, right, preferred_element_type=F4)


def dot_nt(left, right):
    return lax.dot_general(left, right, (((1,), (1,)), ((), ())), preferred_element_type=F4)


def dot_tn(left, right):
    return lax.dot_general(left, right, (((0,), (0,)), ((), ())), preferred_element_type=F4)


def picker(rows, columns, source):
    row = lax.broadcasted_iota(jnp.int32, (rows, columns), 0)
    column = lax.broadcasted_iota(jnp.int32, (rows, columns), 1)
    return jnp.where(column == source(row), 1.0, 0.0).astype(BF)


def fine_source(row):
    kind, m = row // 32, row % 32
    even, odd = 2 * m, 2 * m + 1
    before = jnp.where(m == 0, 64, 2 * m - 1)
    after = jnp.where(m == 31, 65, 2 * m + 2)
    return jnp.where(kind == 0, even, jnp.where(kind == 1, odd, jnp.where(kind == 2, before, after)))


def phase_source(row):
    kind, m = row // 32, row % 32
    before = jnp.where(m == 0, 64, 32 + m - 1)
    after = jnp.where(m == 31, 65, m + 1)
    return jnp.where(kind == 0, before, after)


def weave_source(row):
    return jnp.where(row % 2 == 0, row // 2, 32 + row // 2)


def coarse_source(row):
    shift, m = row // 32, row % 32
    at = m + 2 * shift - 4
    return jnp.where(at < 0, 36 + at, jnp.where(at > 31, 4 + at, at))


def sigmoid(value):
    return 1.0 / (1.0 + jnp.exp(-value))


def fine_rows(slide_ref, top_ref, bottom_ref, lr_ref, shifted, keep=None):
    pick = picker(128, 80, fine_source)

    def put(r, row):
        got = dot(pick, jnp.concatenate([row, lr_ref[r]], axis=0))
        shifted[:, r] = jnp.maximum(got, 0.0).reshape(4, 32, got.shape[1])
        return got

    put(0, top_ref[0])
    put(33, bottom_ref[0])

    def step(i, carry):
        for p in range(2):
            got = put(2 * i + p + 1, slide_ref[2 * i + p])
            if keep is not None:
                keep[2 * p, i] = got[:32].astype(BF)
                keep[2 * p + 1, i] = got[32:64].astype(BF)
        return carry

    lax.fori_loop(0, 16, step, 0, unroll=True)


def fine_conv(i, shifted, taps_ref, flip, put):
    for p in range(2):
        for q in range(2):
            total = None
            for a in range(3):
                for b in range(3):
                    u, v = (2 - a, 2 - b) if flip else (a, b)
                    term = taps_ref[u, v : v + 1, :] * shifted[SOURCE[q][b], 2 * i + p + a]
                    total = term if total is None else total + term
            put(2 * p + q, total)


def fine_forward(
    slide_ref, top_ref, bottom_ref, lr_ref, taps_ref, mix_ref, weight_ref,
    slide_out, depth_out, pre_out, reduced_out, act_out, shifted, total,
):
    fine_rows(slide_ref, top_ref, bottom_ref, lr_ref, shifted, slide_out)

    def conv(i, carry):
        def put(k, value):
            depth_out[k, i] = value.astype(BF)

        fine_conv(i, shifted, taps_ref, False, put)
        return carry

    lax.fori_loop(0, 16, conv, 0, unroll=2)
    chans = mix_ref.shape[0]
    wide = weight_ref.shape[1]
    for k in range(4):
        mixed = dot(depth_out[k].reshape(512, chans), mix_ref[...])
        pre = (slide_out[k].reshape(512, chans).astype(F4) + mixed).astype(BF)
        pre_out[k] = pre
        value = pre.astype(F4)
        unshuffled = (value * sigmoid(value)).astype(BF)
        part = dot(unshuffled, weight_ref[k * chans : (k + 1) * chans, :])
        if k == 0:
            total[...] = part
        else:
            total[...] += part
    reduced = total[...].astype(BF)
    reduced_out[...] = reduced
    value = reduced.astype(F4)
    act_out[...] = (value * sigmoid(value)).astype(BF).reshape(16, 32, wide)


def coarse_rows(row_of, lr_of, shifted):
    pick = picker(160, 48, coarse_source)

    def step(r, carry):
        got = dot(pick, jnp.concatenate([row_of(r), lr_of(r)], axis=0))
        shifted[:, r] = got.reshape(5, 32, got.shape[1])
        return carry

    lax.fori_loop(0, 24, step, 0, unroll=True)


def coarse_backward(
    cot_ref, tb_ref, lr_ref, mixc_ref, tapsc_ref, reduced_ref, deltac_out, delta_red, delta, delta_lr, shiftc
):
    wide = mixc_ref.shape[0]
    mixc = mixc_ref[...]
    inner = dot_nt(cot_ref[...].reshape(512, wide), mixc).astype(BF).reshape(16, 32, wide)
    delta[4:20] = inner
    deltac_out[...] = inner
    edge = dot_nt(tb_ref[...].reshape(256, wide), mixc).astype(BF).reshape(8, 32, wide)
    delta[0:4] = edge[:4]
    delta[20:24] = edge[4:]
    delta_lr[...] = dot_nt(lr_ref[...].reshape(384, wide), mixc).astype(BF).reshape(24, 16, wide)
    coarse_rows(lambda r: delta[r], lambda r: delta_lr[r], shiftc)

    def conv(i, carry):
        total = None
        for a in range(5):
            for b in range(5):
                term = tapsc_ref[4 - a, 4 - b : 5 - b, :] * shiftc[b, i + 2 * a]
                total = term if total is None else total + term
        back = total.astype(BF).astype(F4)
        value = reduced_ref[i].astype(F4)
        s = sigmoid(value)
        slope = s * (1.0 + value * (1.0 - s))
        delta_red[i] = (cot_ref[i].astype(F4) + back * slope).astype(BF)
        return carry

    lax.fori_loop(0, 16, conv, 0, unroll=2)


def fine_terms(
    red_ref, pre_ref, depth_ref, weight_ref, mix_ref, slide_ref, top_ref, bottom_ref, lrf_ref,
    dfine_out, ddepth_out, gred_out, gmix_out, gtaps_out, shifted,
):
    chans = mix_ref.shape[0]
    fine_rows(slide_ref, top_ref, bottom_ref, lrf_ref, shifted)
    red = red_ref[...]
    for k in range(4):
        value = pre_ref[k].astype(F4)
        s = sigmoid(value)
        unshuffled = (value * s).astype(BF)
        gred_out[k * chans : (k + 1) * chans, :] = dot_tn(unshuffled, red).astype(BF)
        spread = dot_nt(red, weight_ref[k * chans : (k + 1) * chans, :])
        dfine = (spread * (s * (1.0 + value * (1.0 - s)))).astype(BF)
        dfine_out[k] = dfine.reshape(16, 32, chans)
        part = dot_tn(depth_ref[k], dfine)
        if k == 0:
            gmix_out[...] = part
        else:
            gmix_out[...] += part
        ddepth_out[k] = dot_nt(dfine, mix_ref[...]).astype(BF).reshape(16, 32, chans)

    def taps(i, sums):
        for p in range(2):
            for q in range(2):
                grad = ddepth_out[2 * p + q, i].astype(F4)
                fresh = []
                for a in range(3):
                    for b in range(3):
                        term = grad * shifted[SOURCE[q][b], 2 * i + p + a]
                        fresh.append(sums[3 * a + b] + jnp.sum(term.reshape(4, 8, chans), axis=0))
                sums = tuple(fresh)
        return sums

    sums = lax.fori_loop(0, 16, taps, tuple(jnp.zeros((8, chans), F4) for _ in range(9)), unroll=2)
    gtaps_out[...] = jnp.zeros_like(gtaps_out)
    for at in range(9):
        gtaps_out[at : at + 1, :] = jnp.sum(sums[at], axis=0, keepdims=True)


def coarse_forward(
    act_ref, top_ref, bottom_ref, lr_ref, taps_ref, mix_ref, reduced_ref, cot_ref, deltac_ref,
    gred_ref, gmixf_ref, gtapsf_ref, core_ref,
    section_out, mine_out, other_out, shifted, sums, depth, rows, packed,
):
    wide = mix_ref.shape[0]
    rows[0:4] = top_ref[...]
    rows[4:20] = act_ref[...]
    rows[20:24] = bottom_ref[...]
    coarse_rows(lambda r: rows[r], lambda r: lr_ref[r], shifted)
    sums[...] = jnp.zeros_like(sums)

    def conv(i, carry):
        total = None
        grad = deltac_ref[i].astype(F4)
        for a in range(5):
            for b in range(5):
                at = 5 * a + b
                window = shifted[b, i + 2 * a]
                term = taps_ref[a, b : b + 1, :] * window
                total = term if total is None else total + term
                sums[at] += jnp.sum((grad * window).reshape(4, 8, wide), axis=0)
        depth[i] = total.astype(BF)
        return carry

    lax.fori_loop(0, 16, conv, 0, unroll=2)
    flat = depth[...].reshape(512, wide)
    section_out[...] = (reduced_ref[...].reshape(512, wide).astype(F4) + dot(flat, mix_ref[...])).astype(BF).reshape(16, 32, wide)
    fine = gmixf_ref.shape[0]
    packed[...] = jnp.zeros_like(packed)
    packed[RED:MIXC, 0:wide] = gred_ref[...]
    packed[MIXC:MIXF, 0:wide] = dot_tn(flat, cot_ref[...].reshape(512, wide)).astype(BF)
    packed[MIXF:TAPC, 0:fine] = gmixf_ref[...].astype(BF)
    taps = jnp.concatenate([jnp.sum(sums[...], axis=1), jnp.zeros((7, wide), F4)], axis=0)
    packed[TAPC:TAPF, 0:wide] = taps.astype(BF)
    packed[TAPF : TAPF + 16, 0:fine] = gtapsf_ref[...].astype(BF)
    core = core_ref[0]
    half = TOTAL // 2
    mine_out[...] = packed[pl.ds(pl.multiple_of(core * half, half), half), :]
    other_out[...] = packed[pl.ds(pl.multiple_of((1 - core) * half, half), half), :]


def unpack(
    near_ref, far_ref, core_ref, tapsf_out, mixf_out, red_out, tapsc_out, mixc_out, packed, *, fine, coarse
):
    core = core_ref[0]
    half = TOTAL // 2
    packed[pl.ds(pl.multiple_of(core * half, half), half), :] = near_ref[...]
    packed[pl.ds(pl.multiple_of((1 - core) * half, half), half), :] = far_ref[...]
    chans = mixf_out.shape[0]
    wide = mixc_out.shape[0]
    red_out[...] = (packed[RED:MIXC, 0:wide].astype(F4) * coarse).T
    mixc_out[...] = packed[MIXC:MIXF, 0:wide].astype(F4) * coarse
    mixf_out[...] = packed[MIXF:TAPC, 0:chans].astype(F4) * fine
    taps = packed[TAPC:TAPF, 0:wide].astype(F4) * coarse
    for a in range(5):
        tapsc_out[a] = taps[5 * a : 5 * a + 5]
    taps = packed[TAPF : TAPF + 16, 0:chans].astype(F4) * fine
    for a in range(3):
        tapsf_out[a] = taps[3 * a : 3 * a + 3]


def fine_backward(
    ddepth_ref, top_ref, bottom_ref, lr_ref, taps_ref, dfine_ref, slide_ref, out_ref, shifted
):
    chans = taps_ref.shape[2]
    pick = picker(64, 80, phase_source)
    weave = picker(64, 64, weave_source)

    def put(r, even, odd):
        got = dot(pick, jnp.concatenate([even, odd, lr_ref[r]], axis=0))
        shifted[0, r] = even.astype(F4)
        shifted[1, r] = odd.astype(F4)
        shifted[2, r] = got[:32]
        shifted[3, r] = got[32:]

    put(0, top_ref[0], top_ref[1])
    put(33, bottom_ref[0], bottom_ref[1])

    def fill(i, carry):
        for p in range(2):
            put(2 * i + p + 1, ddepth_ref[2 * p, i], ddepth_ref[2 * p + 1, i])
        return carry

    lax.fori_loop(0, 16, fill, 0, unroll=True)

    def conv(i, carry):
        found = {}

        def put_one(k, value):
            slide = slide_ref[k, i].astype(F4)
            kept = jnp.where(slide > 0, value, 0.0)
            found[k] = (dfine_ref[k, i].astype(F4) + kept).astype(BF)

        fine_conv(i, shifted, taps_ref, True, put_one)
        for p in range(2):
            both = jnp.concatenate([found[2 * p], found[2 * p + 1]], axis=0)
            out_ref[2 * i + p] = dot(weave, both).astype(BF)
        return carry

    lax.fori_loop(0, 16, conv, 0, unroll=2)


def call(body, outs, scratch, flops, *operands):
    def spec(kind):
        return pl.BlockSpec(memory_space=pltpu.SMEM if kind == jnp.int32 else pltpu.VMEM)

    return pl.pallas_call(
        body,
        out_shape=[jax.ShapeDtypeStruct(shape, kind) for shape, kind in outs],
        in_specs=[spec(operand.dtype) for operand in operands],
        out_specs=[spec(kind) for _, kind in outs],
        scratch_shapes=[pltpu.VMEM(shape, kind) for shape, kind in scratch],
        compiler_params=pltpu.CompilerParams(vmem_limit_bytes=LIMIT),
        cost_estimate=pl.CostEstimate(flops=flops, bytes_accessed=8_000_000, transcendentals=0),
    )(*operands)


def swap(first, last, axes):
    count = lax.axis_size(axes)
    even = lax.axis_index(axes) % 2 == 0
    near = lax.ppermute(jnp.where(even, last, first), axes, [(i, i ^ 1) for i in range(count)])
    far = [(i, i + 1) for i in range(1, count - 1, 2)]
    far = far + [(j, i) for i, j in far]
    away = lax.ppermute(jnp.where(even, first, last), axes, far)
    return jnp.where(even, away, near), jnp.where(even, near, away)


def coarse_edges(coarse):
    height, breadth, wide = coarse.shape
    return coarse[:4].reshape(4 * breadth, wide), coarse[-4:].reshape(4 * breadth, wide)


def coarse_columns(top, coarse, bottom):
    breadth = coarse.shape[1]

    def pick(at):
        parts = [
            jnp.concatenate([top[:, at + s], coarse[:, at + s], bottom[:, at + s]], axis=0)
            for s in range(4)
        ]
        return jnp.concatenate(parts, axis=0)

    return pick(0), pick(breadth - 4)


def coarse_sides(left, right):
    wide = left.shape[1]

    def spread(block):
        return block.reshape(4, -1, wide).transpose(1, 0, 2)

    return sides(spread(left), spread(right))


def fine_columns(low, pixels_left, pixels_right, high):
    end = low.shape[0] - 1
    left = jnp.concatenate([low[:1], pixels_left, high[:1]], axis=0)
    right = jnp.concatenate([low[end:], pixels_right, high[end:]], axis=0)
    return left, right


def fine_sides(left, right):
    return sides(left[:, None], right[:, None])


def stack_rows(coarse, fine):
    widened = jnp.pad(fine, ((0, 0), (0, coarse.shape[1] - fine.shape[1])))
    return jnp.concatenate([coarse, widened], axis=0)


def input_halos(coarse, fine):
    height, breadth, wide = coarse.shape
    chans = fine.shape[-1]
    first, last = coarse_edges(coarse)
    split = 4 * breadth
    low, high = swap(stack_rows(first, fine[0]), stack_rows(last, fine[-1]), ROWS)
    top, bottom = low[:split].reshape(4, breadth, wide), high[:split].reshape(4, breadth, wide)
    fine_low, fine_high = low[split:, :chans], high[split:, :chans]
    coarse_first, coarse_last = coarse_columns(top, coarse, bottom)
    fine_first, fine_last = fine_columns(fine_low, fine[:, 0], fine[:, -1], fine_high)
    left, right = swap(
        stack_rows(coarse_first, fine_first), stack_rows(coarse_last, fine_last), COLS
    )
    split = 4 * (height + 8)
    side_coarse = coarse_sides(left[:split], right[:split])
    side_fine = fine_sides(left[split:, :chans], right[split:, :chans])
    return top, bottom, side_coarse, fine_low, fine_high, side_fine


def hold(value, *others):
    return lax.optimization_barrier((value, *others))[0]


def reduce_terms(mine, other, rows_step, columns_step, last_step):
    total, lanes = mine.shape
    core = lax.axis_index("core")
    plane = lax.axis_size(PLANE)
    depth = lax.axis_size("z")
    trade = [(0, 1), (1, 0)]
    mine = mine + lax.ppermute(other, "core", trade)
    chunk = total // plane
    mine = mine.reshape(plane, chunk, lanes)
    edges = rows_step(mine)
    got = lax.all_to_all(mine, PLANE, 0, 0, tiled=True)
    mine = jnp.sum(got.astype(F4), axis=0).astype(BF)
    mine, edges = lax.optimization_barrier((mine, edges))
    edges = columns_step(edges)
    got = lax.all_to_all(jnp.broadcast_to(mine, (depth, chunk, lanes)), "z", 0, 0, tiled=True)
    mine = jnp.sum(got.astype(F4), axis=0).astype(BF)
    mine, edges = lax.optimization_barrier((mine, edges))
    extra = last_step(edges)
    got = lax.all_to_all(jnp.broadcast_to(mine, (plane, chunk, lanes)), PLANE, 0, 0, tiled=True)
    got, extra = lax.optimization_barrier((got.reshape(total, lanes), extra))
    return got, lax.ppermute(got, "core", trade), extra


def sides(left, right):
    both = jnp.concatenate([left, right], axis=1)
    return jnp.pad(both, ((0, 0), (0, 16 - both.shape[1]), (0, 0)))


def shards(slide_pixels, taps_fine, mix_fine, reduce_weight, taps_coarse, mix_coarse, cotangent):
    height, breadth, chans = slide_pixels.shape
    wide = cotangent.shape[2]
    devices_all = lax.axis_size(ROWS) * lax.axis_size(COLS)
    scale_fine = float(height * breadth * devices_all) ** (-0.5)
    scale_coarse = float(height * breadth // 4 * devices_all) ** (-0.5)
    core = lax.axis_index("core").astype(jnp.int32).reshape(1)
    ctop, cbottom, clr, top, bottom, lr = input_halos(cotangent, slide_pixels)
    top, bottom = top[None], bottom[None]

    slide, depth, pre, reduced, act = call(
        fine_forward,
        [
            ((4, 16, 32, chans), BF),
            ((4, 16, 32, chans), BF),
            ((4, 512, chans), BF),
            ((512, wide), BF),
            ((16, 32, wide), BF),
        ],
        [((4, 34, 32, chans), F4), ((512, wide), F4)],
        4_000_000_000,
        slide_pixels, top, bottom, lr, taps_fine, mix_fine, reduce_weight,
    )
    reduced = reduced.reshape(16, 32, wide)

    delta_coarse, delta_reduced = call(
        coarse_backward,
        [((16, 32, wide), BF), ((16, 32, wide), BF)],
        [((24, 32, wide), BF), ((24, 16, wide), BF), ((5, 24, 32, wide), F4)],
        8_000_000_000,
        cotangent, jnp.concatenate([ctop, cbottom], axis=0), clr, mix_coarse, taps_coarse, reduced,
    )
    arows = swap(*coarse_edges(act), ROWS)
    arows, delta_reduced = lax.optimization_barrier((arows, delta_reduced))
    atop, abottom = (block.reshape(4, 32, wide) for block in arows)
    acolumns = swap(*coarse_columns(atop, act, abottom), COLS)
    dfine, ddepth, term_reduce, term_mix_fine, term_taps_fine = call(
        fine_terms,
        [
            ((4, 16, 32, chans), BF),
            ((4, 16, 32, chans), BF),
            ((4 * chans, wide), BF),
            ((chans, chans), F4),
            ((16, chans), F4),
        ],
        [((4, 34, 32, chans), F4)],
        8_000_000_000,
        delta_reduced.reshape(512, wide), pre, depth.reshape(4, 512, chans), reduce_weight, mix_fine,
        slide_pixels, top, bottom, lr,
    )
    acolumns, ddepth = lax.optimization_barrier((acolumns, ddepth))
    alr = coarse_sides(*acolumns)
    section_out, mine, other = call(
        coarse_forward,
        [((16, 32, wide), BF), ((TOTAL // 2, LANES), BF), ((TOTAL // 2, LANES), BF)],
        [
            ((5, 24, 32, wide), F4),
            ((25, 8, wide), F4),
            ((16, 32, wide), BF),
            ((24, 32, wide), BF),
            ((TOTAL, LANES), BF),
        ],
        4_000_000_000,
        act, atop, abottom, alr, taps_coarse, mix_coarse, reduced, cotangent, delta_coarse,
        term_reduce, term_mix_fine, term_taps_fine, core,
    )
    def rows_step(after):
        edges = ddepth[:2, 0].reshape(breadth, chans), ddepth[2:, 15].reshape(breadth, chans)
        return swap(*hold(edges, after), ROWS)

    def columns_step(edges):
        inner = ddepth.reshape(2, 2, 16, 32, chans)
        left = inner[:, 0, :, 0].transpose(1, 0, 2).reshape(height, chans)
        right = inner[:, 1, :, 31].transpose(1, 0, 2).reshape(height, chans)
        low, high = edges
        return low, high, *swap(*fine_columns(low, left, right, high), COLS)

    def last_step(edges):
        low, high, left, right = edges
        return call(
            fine_backward,
            [((height, breadth, chans), BF)],
            [((4, 34, 32, chans), F4)],
            2_000_000_000,
            ddepth, low.reshape(2, 32, chans), high.reshape(2, 32, chans), fine_sides(left, right),
            taps_fine, dfine, slide,
        )[0]

    near, far, pixel_grad = reduce_terms(mine, other, rows_step, columns_step, last_step)
    grads = call(
        functools.partial(unpack, fine=scale_fine, coarse=scale_coarse),
        [
            ((3, 3, chans), F4),
            ((chans, chans), F4),
            ((wide, 4 * chans), F4),
            ((5, 5, wide), F4),
            ((wide, wide), F4),
        ],
        [((TOTAL, LANES), BF)],
        1_000_000,
        near, far, core,
    )
    tapsf, mixf, red, tapsc, mixc = grads
    return (section_out, pixel_grad, tapsf, mixf, red.T, tapsc, mixc)


def solution(mesh):
    fine = Mesh(mesh.devices.reshape(2, 2, 4, 2, 8), ("yl", "core", "x", "yh", "z"))
    tiles = P(ROWS, COLS, None)
    return jax.shard_map(
        shards,
        mesh=fine,
        in_specs=(tiles, P(), P(), P(), P(), P(), tiles),
        out_specs=(tiles, tiles, P(), P(), P(), P(), P()),
        check_vma=False,
    )
```

```python
import functools

import jax
import jax.numpy as jnp
from jax import lax
from jax.experimental import pallas as pl
from jax.experimental.pallas import tpu as pltpu
from jax.sharding import Mesh, PartitionSpec as P

ROWS = ("yl", "core")
COLS = ("x", "yh", "z")
PLANE = ("yl", "x", "yh")
BF = jnp.bfloat16
F4 = jnp.float32
LIMIT = 28 * 1024 * 1024
RED, MIXC, MIXF, TAPC, TAPF, TOTAL = 0, 832, 1248, 1456, 1488, 1536
LANES = 512
SOURCE = ((2, 0, 1), (0, 1, 3))


def dot(left, right):
    return jnp.dot(left, right, preferred_element_type=F4)


def dot_nt(left, right):
    return lax.dot_general(left, right, (((1,), (1,)), ((), ())), preferred_element_type=F4)


def dot_tn(left, right):
    return lax.dot_general(left, right, (((0,), (0,)), ((), ())), preferred_element_type=F4)


def picker(rows, columns, source):
    row = lax.broadcasted_iota(jnp.int32, (rows, columns), 0)
    column = lax.broadcasted_iota(jnp.int32, (rows, columns), 1)
    return jnp.where(column == source(row), 1.0, 0.0).astype(BF)


def fine_source(row):
    kind, m = row // 32, row % 32
    even, odd = 2 * m, 2 * m + 1
    before = jnp.where(m == 0, 64, 2 * m - 1)
    after = jnp.where(m == 31, 65, 2 * m + 2)
    return jnp.where(kind == 0, even, jnp.where(kind == 1, odd, jnp.where(kind == 2, before, after)))


def phase_source(row):
    kind, m = row // 32, row % 32
    before = jnp.where(m == 0, 64, 32 + m - 1)
    after = jnp.where(m == 31, 65, m + 1)
    return jnp.where(kind == 0, before, after)


def weave_source(row):
    return jnp.where(row % 2 == 0, row // 2, 32 + row // 2)


def coarse_source(row):
    shift, m = row // 32, row % 32
    at = m + 2 * shift - 4
    return jnp.where(at < 0, 36 + at, jnp.where(at > 31, 4 + at, at))


def sigmoid(value):
    return 0.5 * jnp.tanh(0.5 * value) + 0.5


def fine_rows(slide_ref, top_ref, bottom_ref, lr_ref, shifted, keep=None):
    pick = picker(128, 80, fine_source)

    def put(r, row):
        got = dot(pick, jnp.concatenate([row, lr_ref[r]], axis=0))
        shifted[:, r] = jnp.maximum(got, 0.0).reshape(4, 32, got.shape[1])
        return got

    put(0, top_ref[0])
    put(33, bottom_ref[0])

    def step(i, carry):
        for p in range(2):
            got = put(2 * i + p + 1, slide_ref[2 * i + p])
            if keep is not None:
                keep[2 * p, i] = got[:32].astype(BF)
                keep[2 * p + 1, i] = got[32:64].astype(BF)
        return carry

    lax.fori_loop(0, 16, step, 0, unroll=True)


def fine_conv(i, shifted, taps_ref, flip, put):
    for p in range(2):
        for q in range(2):
            total = None
            for a in range(3):
                for b in range(3):
                    u, v = (2 - a, 2 - b) if flip else (a, b)
                    term = taps_ref[u, v : v + 1, :] * shifted[SOURCE[q][b], 2 * i + p + a]
                    total = term if total is None else total + term
            put(2 * p + q, total)


def fine_forward(
    slide_ref, top_ref, bottom_ref, lr_ref, taps_ref, mix_ref, weight_ref,
    slide_out, depth_out, pre_out, reduced_out, act_out, shifted, total,
):
    fine_rows(slide_ref, top_ref, bottom_ref, lr_ref, shifted, slide_out)

    def conv(i, carry):
        def put(k, value):
            depth_out[k, i] = value.astype(BF)

        fine_conv(i, shifted, taps_ref, False, put)
        return carry

    lax.fori_loop(0, 16, conv, 0, unroll=2)
    chans = mix_ref.shape[0]
    wide = weight_ref.shape[1]
    for k in range(4):
        mixed = dot(depth_out[k].reshape(512, chans), mix_ref[...])
        pre = (slide_out[k].reshape(512, chans).astype(F4) + mixed).astype(BF)
        pre_out[k] = pre
        value = pre.astype(F4)
        unshuffled = (value * sigmoid(value)).astype(BF)
        part = dot(unshuffled, weight_ref[k * chans : (k + 1) * chans, :])
        if k == 0:
            total[...] = part
        else:
            total[...] += part
    reduced = total[...].astype(BF)
    reduced_out[...] = reduced
    value = reduced.astype(F4)
    act_out[...] = (value * sigmoid(value)).astype(BF).reshape(16, 32, wide)


def coarse_rows(row_of, lr_of, shifted):
    pick = picker(160, 48, coarse_source)

    def step(r, carry):
        got = dot(pick, jnp.concatenate([row_of(r), lr_of(r)], axis=0))
        shifted[:, r] = got.reshape(5, 32, got.shape[1])
        return carry

    lax.fori_loop(0, 24, step, 0, unroll=True)


def coarse_backward(
    cot_ref, tb_ref, lr_ref, mixc_ref, tapsc_ref, reduced_ref, deltac_out, delta_red, delta, delta_lr, shiftc
):
    wide = mixc_ref.shape[0]
    mixc = mixc_ref[...]
    inner = dot_nt(cot_ref[...].reshape(512, wide), mixc).astype(BF).reshape(16, 32, wide)
    delta[4:20] = inner
    deltac_out[...] = inner
    edge = dot_nt(tb_ref[...].reshape(256, wide), mixc).astype(BF).reshape(8, 32, wide)
    delta[0:4] = edge[:4]
    delta[20:24] = edge[4:]
    delta_lr[...] = dot_nt(lr_ref[...].reshape(384, wide), mixc).astype(BF).reshape(24, 16, wide)
    coarse_rows(lambda r: delta[r], lambda r: delta_lr[r], shiftc)

    def conv(i, carry):
        total = None
        for a in range(5):
            for b in range(5):
                term = tapsc_ref[4 - a, 4 - b : 5 - b, :] * shiftc[b, i + 2 * a]
                total = term if total is None else total + term
        back = total.astype(BF).astype(F4)
        value = reduced_ref[i].astype(F4)
        s = sigmoid(value)
        slope = s * (1.0 + value * (1.0 - s))
        delta_red[i] = (cot_ref[i].astype(F4) + back * slope).astype(BF)
        return carry

    lax.fori_loop(0, 16, conv, 0, unroll=2)


def fine_terms(
    red_ref, pre_ref, depth_ref, weight_ref, mix_ref, slide_ref, top_ref, bottom_ref, lrf_ref,
    dfine_out, ddepth_out, gred_out, gmix_out, gtaps_out, shifted,
):
    chans = mix_ref.shape[0]
    fine_rows(slide_ref, top_ref, bottom_ref, lrf_ref, shifted)
    red = red_ref[...]
    for k in range(4):
        value = pre_ref[k].astype(F4)
        s = sigmoid(value)
        unshuffled = (value * s).astype(BF)
        gred_out[k * chans : (k + 1) * chans, :] = dot_tn(unshuffled, red).astype(BF)
        spread = dot_nt(red, weight_ref[k * chans : (k + 1) * chans, :])
        dfine = (spread * (s * (1.0 + value * (1.0 - s)))).astype(BF)
        dfine_out[k] = dfine.reshape(16, 32, chans)
        part = dot_tn(depth_ref[k], dfine)
        if k == 0:
            gmix_out[...] = part
        else:
            gmix_out[...] += part
        ddepth_out[k] = dot_nt(dfine, mix_ref[...]).astype(BF).reshape(16, 32, chans)

    def taps(i, sums):
        for p in range(2):
            for q in range(2):
                grad = ddepth_out[2 * p + q, i].astype(F4)
                fresh = []
                for a in range(3):
                    for b in range(3):
                        term = grad * shifted[SOURCE[q][b], 2 * i + p + a]
                        fresh.append(sums[3 * a + b] + jnp.sum(term.reshape(4, 8, chans), axis=0))
                sums = tuple(fresh)
        return sums

    sums = lax.fori_loop(0, 16, taps, tuple(jnp.zeros((8, chans), F4) for _ in range(9)), unroll=2)
    gtaps_out[...] = jnp.zeros_like(gtaps_out)
    for at in range(9):
        gtaps_out[at : at + 1, :] = jnp.sum(sums[at], axis=0, keepdims=True)


def edge_message(outs, source, bases, ats, near_ref, away_ref, middle):
    for out, at in zip(outs, ats):
        total = 0.0
        for block, base in ((near_ref[...], bases[0]), (away_ref[...], bases[1]), (middle, None)):
            pick = picker(out.shape[0], block.shape[0], functools.partial(source, at, base))
            total = total + dot(pick, block)
        out[...] = total.astype(BF)


def coarse_message(flags_ref, near_ref, away_ref, act_ref, near_out, away_out):
    def source(at, base, row):
        column, r = row // 24, row % 24
        if base is None:
            inside = jnp.logical_and(r >= 4, r < 20)
            return jnp.where(inside, (r - 4) * 32 + at + column, -1)
        inside = jnp.logical_and(r >= base, r < base + 4)
        return jnp.where(inside, (r - base) * 32 + at + column, -1)

    base = jnp.where(flags_ref[0] == 0, 20, 0)
    at = jnp.where(flags_ref[1] == 0, 28, 0)
    middle = act_ref[...].reshape(512, act_ref.shape[2])
    edge_message((near_out, away_out), source, (base, 20 - base), (at, 28 - at), near_ref, away_ref, middle)


def fine_message(flags_ref, near_ref, away_ref, ddepth_ref, near_out, away_out):
    def source(at, base, row):
        if base is None:
            r = row - 1
            inside = jnp.logical_and(r >= 0, r < 32)
            return jnp.where(inside, ((r % 2) * 32 + r // 2) * 32 + at * 543, -1)
        return jnp.where(row == base, at * 63, -1)

    base = jnp.where(flags_ref[0] == 0, 33, 0)
    at = jnp.where(flags_ref[1] == 0, 1, 0)
    middle = ddepth_ref[...].reshape(2048, ddepth_ref.shape[3])
    edge_message((near_out, away_out), source, (base, 33 - base), (at, 1 - at), near_ref, away_ref, middle)


def side_rows(flags_ref, near_ref, away_ref, rows, width):
    def source(base, row):
        r, place = row // 16, row % 16 - base
        inside = jnp.logical_and(place >= 0, place < width)
        return jnp.where(inside, place * rows + r, -1)

    base = jnp.where(flags_ref[1] == 0, width, 0)
    total = 0.0
    for block, at in ((near_ref[...], base), (away_ref[...], width - base)):
        pick = picker(16 * rows, block.shape[0], functools.partial(source, at))
        total = total + dot(pick, block)
    return total.astype(BF).reshape(rows, 16, near_ref.shape[1])


def coarse_forward(
    flags_ref, act_ref, near_ref, away_ref, nside_ref, aside_ref, taps_ref, mix_ref, reduced_ref, cot_ref, deltac_ref,
    gred_ref, gmixf_ref, gtapsf_ref,
    section_out, mine_out, other_out, shifted, sums, depth, rows, sides_of, packed,
):
    wide = mix_ref.shape[0]
    for parity in range(2):

        @pl.when(flags_ref[0] == parity)
        def _():
            low, high = (near_ref, away_ref) if parity else (away_ref, near_ref)
            rows[0:4] = low[...].reshape(4, 32, wide)
            rows[20:24] = high[...].reshape(4, 32, wide)

    rows[4:20] = act_ref[...]
    sides_of[...] = side_rows(flags_ref, nside_ref, aside_ref, 24, 4)
    coarse_rows(lambda r: rows[r], lambda r: sides_of[r], shifted)
    sums[...] = jnp.zeros_like(sums)

    def conv(i, carry):
        total = None
        grad = deltac_ref[i].astype(F4)
        for a in range(5):
            for b in range(5):
                at = 5 * a + b
                window = shifted[b, i + 2 * a]
                term = taps_ref[a, b : b + 1, :] * window
                total = term if total is None else total + term
                sums[at] += jnp.sum((grad * window).reshape(4, 8, wide), axis=0)
        depth[i] = total.astype(BF)
        return carry

    lax.fori_loop(0, 16, conv, 0, unroll=2)
    flat = depth[...].reshape(512, wide)
    section_out[...] = (reduced_ref[...].reshape(512, wide).astype(F4) + dot(flat, mix_ref[...])).astype(BF).reshape(16, 32, wide)
    fine = gmixf_ref.shape[0]
    packed[...] = jnp.zeros_like(packed)
    packed[RED:MIXC, 0:wide] = gred_ref[...]
    packed[MIXC:MIXF, 0:wide] = dot_tn(flat, cot_ref[...].reshape(512, wide)).astype(BF)
    packed[MIXF:TAPC, 0:fine] = gmixf_ref[...].astype(BF)
    taps = jnp.concatenate([jnp.sum(sums[...], axis=1), jnp.zeros((7, wide), F4)], axis=0)
    packed[TAPC:TAPF, 0:wide] = taps.astype(BF)
    packed[TAPF : TAPF + 16, 0:fine] = gtapsf_ref[...].astype(BF)
    core = flags_ref[2]
    half = TOTAL // 2
    mine_out[...] = packed[pl.ds(pl.multiple_of(core * half, half), half), :]
    other_out[...] = packed[pl.ds(pl.multiple_of((1 - core) * half, half), half), :]


def unpack(
    flags_ref, near_ref, far_ref, tapsf_out, mixf_out, red_out, tapsc_out, mixc_out, packed, *, fine, coarse
):
    core = flags_ref[2]
    half = TOTAL // 2
    packed[pl.ds(pl.multiple_of(core * half, half), half), :] = near_ref[...]
    packed[pl.ds(pl.multiple_of((1 - core) * half, half), half), :] = far_ref[...]
    chans = mixf_out.shape[0]
    wide = mixc_out.shape[0]
    red_out[...] = (packed[RED:MIXC, 0:wide].astype(F4) * coarse).T
    mixc_out[...] = packed[MIXC:MIXF, 0:wide].astype(F4) * coarse
    mixf_out[...] = packed[MIXF:TAPC, 0:chans].astype(F4) * fine
    taps = packed[TAPC:TAPF, 0:wide].astype(F4) * coarse
    for a in range(5):
        tapsc_out[a] = taps[5 * a : 5 * a + 5]
    taps = packed[TAPF : TAPF + 16, 0:chans].astype(F4) * fine
    for a in range(3):
        tapsf_out[a] = taps[3 * a : 3 * a + 3]


def fine_backward(
    flags_ref, ddepth_ref, near_ref, away_ref, nside_ref, aside_ref, taps_ref, dfine_ref, slide_ref, out_ref,
    shifted, lr_ref, ends,
):
    chans = taps_ref.shape[2]
    pick = picker(64, 80, phase_source)
    weave = picker(64, 64, weave_source)

    def put(r, even, odd):
        got = dot(pick, jnp.concatenate([even, odd, lr_ref[r]], axis=0))
        shifted[0, r] = even.astype(F4)
        shifted[1, r] = odd.astype(F4)
        shifted[2, r] = got[:32]
        shifted[3, r] = got[32:]

    lr_ref[...] = side_rows(flags_ref, nside_ref, aside_ref, 48, 1)
    for parity in range(2):

        @pl.when(flags_ref[0] == parity)
        def _():
            low, high = (near_ref, away_ref) if parity else (away_ref, near_ref)
            ends[0] = low[...]
            ends[1] = high[...]

    put(0, ends[0, :32], ends[0, 32:])
    put(33, ends[1, :32], ends[1, 32:])

    def fill(i, carry):
        for p in range(2):
            put(2 * i + p + 1, ddepth_ref[2 * p, i], ddepth_ref[2 * p + 1, i])
        return carry

    lax.fori_loop(0, 16, fill, 0, unroll=True)

    def conv(i, carry):
        found = {}

        def put_one(k, value):
            slide = slide_ref[k, i].astype(F4)
            kept = jnp.where(slide > 0, value, 0.0)
            found[k] = (dfine_ref[k, i].astype(F4) + kept).astype(BF)

        fine_conv(i, shifted, taps_ref, True, put_one)
        for p in range(2):
            both = jnp.concatenate([found[2 * p], found[2 * p + 1]], axis=0)
            out_ref[2 * i + p] = dot(weave, both).astype(BF)
        return carry

    lax.fori_loop(0, 16, conv, 0, unroll=2)


def call(body, outs, scratch, flops, *operands):
    def spec(kind):
        return pl.BlockSpec(memory_space=pltpu.SMEM if kind == jnp.int32 else pltpu.VMEM)

    return pl.pallas_call(
        body,
        out_shape=[jax.ShapeDtypeStruct(shape, kind) for shape, kind in outs],
        in_specs=[spec(operand.dtype) for operand in operands],
        out_specs=[spec(kind) for _, kind in outs],
        scratch_shapes=[pltpu.VMEM(shape, kind) for shape, kind in scratch],
        compiler_params=pltpu.CompilerParams(vmem_limit_bytes=LIMIT),
        cost_estimate=pl.CostEstimate(flops=flops, bytes_accessed=8_000_000, transcendentals=0),
    )(*operands)


def trade(first, last, axes):
    even = lax.axis_index(axes) % 2 == 0
    return send(jnp.where(even, last, first), jnp.where(even, first, last), axes)


def send(near, away, axes):
    count = lax.axis_size(axes)
    far = [(i, i + 1) for i in range(1, count - 1, 2)]
    far = far + [(j, i) for i, j in far]
    return (
        lax.ppermute(near, axes, [(i, i ^ 1) for i in range(count)]),
        lax.ppermute(away, axes, far),
    )


def swap(first, last, axes):
    even = lax.axis_index(axes) % 2 == 0
    near, away = trade(first, last, axes)
    return jnp.where(even, away, near), jnp.where(even, near, away)


def coarse_edges(coarse):
    height, breadth, wide = coarse.shape
    return coarse[:4].reshape(4 * breadth, wide), coarse[-4:].reshape(4 * breadth, wide)


def coarse_columns(top, coarse, bottom):
    breadth = coarse.shape[1]

    def pick(at):
        parts = [
            jnp.concatenate([top[:, at + s], coarse[:, at + s], bottom[:, at + s]], axis=0)
            for s in range(4)
        ]
        return jnp.concatenate(parts, axis=0)

    return pick(0), pick(breadth - 4)


def coarse_sides(left, right):
    wide = left.shape[1]

    def spread(block):
        return block.reshape(4, -1, wide).transpose(1, 0, 2)

    return sides(spread(left), spread(right))


def fine_columns(low, pixels_left, pixels_right, high):
    end = low.shape[0] - 1
    left = jnp.concatenate([low[:1], pixels_left, high[:1]], axis=0)
    right = jnp.concatenate([low[end:], pixels_right, high[end:]], axis=0)
    return left, right


def fine_sides(left, right):
    return sides(left[:, None], right[:, None])


def stack_rows(coarse, fine):
    widened = jnp.pad(fine, ((0, 0), (0, coarse.shape[1] - fine.shape[1])))
    return jnp.concatenate([coarse, widened], axis=0)


def input_halos(coarse, fine):
    height, breadth, wide = coarse.shape
    chans = fine.shape[-1]
    first, last = coarse_edges(coarse)
    split = 4 * breadth
    low, high = swap(stack_rows(first, fine[0]), stack_rows(last, fine[-1]), ROWS)
    top, bottom = low[:split].reshape(4, breadth, wide), high[:split].reshape(4, breadth, wide)
    fine_low, fine_high = low[split:, :chans], high[split:, :chans]
    coarse_first, coarse_last = coarse_columns(top, coarse, bottom)
    fine_first, fine_last = fine_columns(fine_low, fine[:, 0], fine[:, -1], fine_high)
    left, right = swap(
        stack_rows(coarse_first, fine_first), stack_rows(coarse_last, fine_last), COLS
    )
    split = 4 * (height + 8)
    side_coarse = coarse_sides(left[:split], right[:split])
    side_fine = fine_sides(left[split:, :chans], right[split:, :chans])
    return top, bottom, side_coarse, fine_low, fine_high, side_fine


def hold(value, *others):
    return lax.optimization_barrier((value, *others))[0]


def reduce_terms(mine, other, rows_step, columns_step, last_step):
    total, lanes = mine.shape
    core = lax.axis_index("core")
    plane = lax.axis_size(PLANE)
    depth = lax.axis_size("z")
    across = [(0, 1), (1, 0)]
    mine = mine + lax.ppermute(other, "core", across)
    chunk = total // plane
    mine = mine.reshape(plane, chunk, lanes)
    edges = rows_step(mine)
    got = lax.all_to_all(mine, PLANE, 0, 0, tiled=True)
    mine = jnp.sum(got.astype(F4), axis=0).astype(BF)
    mine, edges = lax.optimization_barrier((mine, edges))
    edges = columns_step(edges)
    got = lax.all_to_all(jnp.broadcast_to(mine, (depth, chunk, lanes)), "z", 0, 0, tiled=True)
    mine = jnp.sum(got.astype(F4), axis=0).astype(BF)
    mine, edges = lax.optimization_barrier((mine, edges))
    extra = last_step(edges)
    got = lax.all_to_all(jnp.broadcast_to(mine, (plane, chunk, lanes)), PLANE, 0, 0, tiled=True)
    got, extra = lax.optimization_barrier((got.reshape(total, lanes), extra))
    return got, lax.ppermute(got, "core", across), extra


def sides(left, right):
    both = jnp.concatenate([left, right], axis=1)
    return jnp.pad(both, ((0, 0), (0, 16 - both.shape[1]), (0, 0)))


def shards(slide_pixels, taps_fine, mix_fine, reduce_weight, taps_coarse, mix_coarse, cotangent):
    height, breadth, chans = slide_pixels.shape
    wide = cotangent.shape[2]
    devices_all = lax.axis_size(ROWS) * lax.axis_size(COLS)
    scale_fine = float(height * breadth * devices_all) ** (-0.5)
    scale_coarse = float(height * breadth // 4 * devices_all) ** (-0.5)
    flags = jnp.stack(
        [lax.axis_index(ROWS) % 2, lax.axis_index(COLS) % 2, lax.axis_index("core")]
    ).astype(jnp.int32)
    ctop, cbottom, clr, top, bottom, lr = input_halos(cotangent, slide_pixels)
    top, bottom = top[None], bottom[None]

    slide, depth, pre, reduced, act = call(
        fine_forward,
        [
            ((4, 16, 32, chans), BF),
            ((4, 16, 32, chans), BF),
            ((4, 512, chans), BF),
            ((512, wide), BF),
            ((16, 32, wide), BF),
        ],
        [((4, 34, 32, chans), F4), ((512, wide), F4)],
        4_000_000_000,
        slide_pixels, top, bottom, lr, taps_fine, mix_fine, reduce_weight,
    )
    reduced = reduced.reshape(16, 32, wide)

    delta_coarse, delta_reduced = call(
        coarse_backward,
        [((16, 32, wide), BF), ((16, 32, wide), BF)],
        [((24, 32, wide), BF), ((24, 16, wide), BF), ((5, 24, 32, wide), F4)],
        8_000_000_000,
        cotangent, jnp.concatenate([ctop, cbottom], axis=0), clr, mix_coarse, taps_coarse, reduced,
    )
    arows = trade(*coarse_edges(act), ROWS)
    arows, delta_reduced = lax.optimization_barrier((arows, delta_reduced))
    tall = 4 * (height // 2 + 8)
    message = call(
        coarse_message, [((tall, wide), BF), ((tall, wide), BF)], [], 10_000_000, flags, *arows, act
    )
    acolumns = send(*message, COLS)
    dfine, ddepth, term_reduce, term_mix_fine, term_taps_fine = call(
        fine_terms,
        [
            ((4, 16, 32, chans), BF),
            ((4, 16, 32, chans), BF),
            ((4 * chans, wide), BF),
            ((chans, chans), F4),
            ((16, chans), F4),
        ],
        [((4, 34, 32, chans), F4)],
        8_000_000_000,
        delta_reduced.reshape(512, wide), pre, depth.reshape(4, 512, chans), reduce_weight, mix_fine,
        slide_pixels, top, bottom, lr,
    )
    acolumns, ddepth = lax.optimization_barrier((acolumns, ddepth))
    section_out, mine, other = call(
        coarse_forward,
        [((16, 32, wide), BF), ((TOTAL // 2, LANES), BF), ((TOTAL // 2, LANES), BF)],
        [
            ((5, 24, 32, wide), F4),
            ((25, 8, wide), F4),
            ((16, 32, wide), BF),
            ((24, 32, wide), BF),
            ((24, 16, wide), BF),
            ((TOTAL, LANES), BF),
        ],
        4_000_000_000,
        flags, act, *arows, *acolumns, taps_coarse, mix_coarse, reduced, cotangent, delta_coarse,
        term_reduce, term_mix_fine, term_taps_fine,
    )
    def rows_step(after):
        edges = ddepth[:2, 0].reshape(breadth, chans), ddepth[2:, 15].reshape(breadth, chans)
        return trade(*hold(edges, after), ROWS)

    def columns_step(rows):
        message = call(
            fine_message, [((48, chans), BF), ((48, chans), BF)], [], 10_000_000, flags, *rows, ddepth
        )
        return *rows, *send(*message, COLS)

    def last_step(edges):
        return call(
            fine_backward,
            [((height, breadth, chans), BF)],
            [((4, 34, 32, chans), F4), ((48, 16, chans), BF), ((2, 64, chans), BF)],
            2_000_000_000,
            flags, ddepth, *edges, taps_fine, dfine, slide,
        )[0]

    near, far, pixel_grad = reduce_terms(mine, other, rows_step, columns_step, last_step)
    grads = call(
        functools.partial(unpack, fine=scale_fine, coarse=scale_coarse),
        [
            ((3, 3, chans), F4),
            ((chans, chans), F4),
            ((wide, 4 * chans), F4),
            ((5, 5, wide), F4),
            ((wide, wide), F4),
        ],
        [((TOTAL, LANES), BF)],
        1_000_000,
        flags, near, far,
    )
    tapsf, mixf, red, tapsc, mixc = grads
    return (section_out, pixel_grad, tapsf, mixf, red.T, tapsc, mixc)


def solution(mesh):
    fine = Mesh(mesh.devices.reshape(2, 2, 4, 2, 8), ("yl", "core", "x", "yh", "z"))
    tiles = P(ROWS, COLS, None)
    return jax.shard_map(
        shards,
        mesh=fine,
        in_specs=(tiles, P(), P(), P(), P(), P(), tiles),
        out_specs=(tiles, tiles, P(), P(), P(), P(), P()),
        check_vma=False,
    )
```

```python
import functools

import jax
import jax.numpy as jnp
from jax import lax
from jax.experimental import pallas as pl
from jax.experimental.pallas import tpu as pltpu
from jax.sharding import Mesh, PartitionSpec as P

ROWS = ("yl", "core")
COLS = ("x", "yh", "z")
PLANE = ("yl", "x", "yh")
BF = jnp.bfloat16
F4 = jnp.float32
LIMIT = 28 * 1024 * 1024
MIXC, TAPC, TOTAL, FINE = 832, 1248, 1280, 224
LANES = 512
SOURCE = ((2, 0, 1), (0, 1, 3))


def dot(left, right):
    return jnp.dot(left, right, preferred_element_type=F4)


def dot_nt(left, right):
    return lax.dot_general(left, right, (((1,), (1,)), ((), ())), preferred_element_type=F4)


def dot_tn(left, right):
    return lax.dot_general(left, right, (((0,), (0,)), ((), ())), preferred_element_type=F4)


def picker(rows, columns, source):
    row = lax.broadcasted_iota(jnp.int32, (rows, columns), 0)
    column = lax.broadcasted_iota(jnp.int32, (rows, columns), 1)
    return jnp.where(column == source(row), 1.0, 0.0).astype(BF)


def fine_source(row):
    kind, m = row // 32, row % 32
    even, odd = 2 * m, 2 * m + 1
    before = jnp.where(m == 0, 64, 2 * m - 1)
    after = jnp.where(m == 31, 65, 2 * m + 2)
    return jnp.where(kind == 0, even, jnp.where(kind == 1, odd, jnp.where(kind == 2, before, after)))


def phase_source(row):
    kind, m = row // 32, row % 32
    before = jnp.where(m == 0, 64, 32 + m - 1)
    after = jnp.where(m == 31, 65, m + 1)
    return jnp.where(kind == 0, before, after)


def weave_source(row):
    return jnp.where(row % 2 == 0, row // 2, 32 + row // 2)


def coarse_source(row):
    shift, m = row // 32, row % 32
    at = m + 2 * shift - 4
    return jnp.where(at < 0, 36 + at, jnp.where(at > 31, 4 + at, at))


def sigmoid(value):
    return 0.5 * jnp.tanh(0.5 * value) + 0.5


def fine_rows(slide_ref, top_ref, bottom_ref, lr_ref, shifted, keep=None):
    pick = picker(128, 80, fine_source)

    def put(r, row):
        got = dot(pick, jnp.concatenate([row, lr_ref[r]], axis=0))
        shifted[:, r] = jnp.maximum(got, 0.0).reshape(4, 32, got.shape[1])
        return got

    put(0, top_ref[0])
    put(33, bottom_ref[0])

    def step(i, carry):
        for p in range(2):
            got = put(2 * i + p + 1, slide_ref[2 * i + p])
            if keep is not None:
                keep[2 * p, i] = got[:32].astype(BF)
                keep[2 * p + 1, i] = got[32:64].astype(BF)
        return carry

    lax.fori_loop(0, 16, step, 0, unroll=True)


def fine_conv(i, shifted, taps_ref, flip, put):
    for p in range(2):
        for q in range(2):
            total = None
            for a in range(3):
                for b in range(3):
                    u, v = (2 - a, 2 - b) if flip else (a, b)
                    term = taps_ref[u, v : v + 1, :] * shifted[SOURCE[q][b], 2 * i + p + a]
                    total = term if total is None else total + term
            put(2 * p + q, total)


def fine_forward(
    slide_ref, top_ref, bottom_ref, lr_ref, taps_ref, mix_ref, weight_ref,
    slide_out, depth_out, pre_out, reduced_out, act_out, shifted, total,
):
    fine_rows(slide_ref, top_ref, bottom_ref, lr_ref, shifted, slide_out)

    def conv(i, carry):
        def put(k, value):
            depth_out[k, i] = value.astype(BF)

        fine_conv(i, shifted, taps_ref, False, put)
        return carry

    lax.fori_loop(0, 16, conv, 0, unroll=2)
    chans = mix_ref.shape[0]
    wide = weight_ref.shape[1]
    for k in range(4):
        mixed = dot(depth_out[k].reshape(512, chans), mix_ref[...])
        pre = (slide_out[k].reshape(512, chans).astype(F4) + mixed).astype(BF)
        pre_out[k] = pre
        value = pre.astype(F4)
        unshuffled = (value * sigmoid(value)).astype(BF)
        part = dot(unshuffled, weight_ref[k * chans : (k + 1) * chans, :])
        if k == 0:
            total[...] = part
        else:
            total[...] += part
    reduced = total[...].astype(BF)
    reduced_out[...] = reduced
    value = reduced.astype(F4)
    act_out[...] = (value * sigmoid(value)).astype(BF).reshape(16, 32, wide)


def coarse_rows(row_of, lr_of, shifted):
    pick = picker(160, 48, coarse_source)

    def step(r, carry):
        got = dot(pick, jnp.concatenate([row_of(r), lr_of(r)], axis=0))
        shifted[:, r] = got.reshape(5, 32, got.shape[1])
        return carry

    lax.fori_loop(0, 24, step, 0, unroll=True)


def coarse_backward(
    cot_ref, tb_ref, lr_ref, mixc_ref, tapsc_ref, reduced_ref, deltac_out, delta_red, delta, delta_lr, shiftc
):
    wide = mixc_ref.shape[0]
    mixc = mixc_ref[...]
    inner = dot_nt(cot_ref[...].reshape(512, wide), mixc).astype(BF).reshape(16, 32, wide)
    delta[4:20] = inner
    deltac_out[...] = inner
    edge = dot_nt(tb_ref[...].reshape(256, wide), mixc).astype(BF).reshape(8, 32, wide)
    delta[0:4] = edge[:4]
    delta[20:24] = edge[4:]
    delta_lr[...] = dot_nt(lr_ref[...].reshape(384, wide), mixc).astype(BF).reshape(24, 16, wide)
    coarse_rows(lambda r: delta[r], lambda r: delta_lr[r], shiftc)

    def conv(i, carry):
        total = None
        for a in range(5):
            for b in range(5):
                term = tapsc_ref[4 - a, 4 - b : 5 - b, :] * shiftc[b, i + 2 * a]
                total = term if total is None else total + term
        back = total.astype(BF).astype(F4)
        value = reduced_ref[i].astype(F4)
        s = sigmoid(value)
        slope = s * (1.0 + value * (1.0 - s))
        delta_red[i] = (cot_ref[i].astype(F4) + back * slope).astype(BF)
        return carry

    lax.fori_loop(0, 16, conv, 0, unroll=2)


def fine_terms(
    red_ref, pre_ref, depth_ref, weight_ref, mix_ref, slide_ref, top_ref, bottom_ref, lrf_ref,
    dfine_out, ddepth_out, gred_out, gmix_out, gtaps_out, shifted,
):
    chans = mix_ref.shape[0]
    fine_rows(slide_ref, top_ref, bottom_ref, lrf_ref, shifted)
    red = red_ref[...]
    for k in range(4):
        value = pre_ref[k].astype(F4)
        s = sigmoid(value)
        unshuffled = (value * s).astype(BF)
        gred_out[k * chans : (k + 1) * chans, :] = dot_tn(unshuffled, red).astype(BF)
        spread = dot_nt(red, weight_ref[k * chans : (k + 1) * chans, :])
        dfine = (spread * (s * (1.0 + value * (1.0 - s)))).astype(BF)
        dfine_out[k] = dfine.reshape(16, 32, chans)
        part = dot_tn(depth_ref[k], dfine)
        if k == 0:
            gmix_out[...] = part
        else:
            gmix_out[...] += part
        ddepth_out[k] = dot_nt(dfine, mix_ref[...]).astype(BF).reshape(16, 32, chans)

    def taps(i, sums):
        for p in range(2):
            for q in range(2):
                grad = ddepth_out[2 * p + q, i].astype(F4)
                fresh = []
                for a in range(3):
                    for b in range(3):
                        term = grad * shifted[SOURCE[q][b], 2 * i + p + a]
                        fresh.append(sums[3 * a + b] + jnp.sum(term.reshape(4, 8, chans), axis=0))
                sums = tuple(fresh)
        return sums

    sums = lax.fori_loop(0, 16, taps, tuple(jnp.zeros((8, chans), F4) for _ in range(9)), unroll=2)
    gtaps_out[...] = jnp.zeros_like(gtaps_out)
    for at in range(9):
        gtaps_out[at : at + 1, :] = jnp.sum(sums[at], axis=0, keepdims=True)


def piece(j, chans, wide):
    room = LANES - wide
    return picker(
        chans, LANES, lambda row: jnp.where(row // room == j, wide + row % room, -1)
    )


def edge_message(outs, source, bases, ats, near_ref, away_ref, middle):
    for out, at in zip(outs, ats):
        total = 0.0
        for block, base in ((near_ref[...], bases[0]), (away_ref[...], bases[1]), (middle, None)):
            pick = picker(out.shape[0], block.shape[0], functools.partial(source, at, base))
            total = total + dot(pick, block)
        out[...] = total.astype(BF)


def coarse_message(flags_ref, near_ref, away_ref, act_ref, near_out, away_out):
    def source(at, base, row):
        column, r = row // 24, row % 24
        if base is None:
            inside = jnp.logical_and(r >= 4, r < 20)
            return jnp.where(inside, (r - 4) * 32 + at + column, -1)
        inside = jnp.logical_and(r >= base, r < base + 4)
        return jnp.where(inside, (r - base) * 32 + at + column, -1)

    base = jnp.where(flags_ref[0] == 0, 20, 0)
    at = jnp.where(flags_ref[1] == 0, 28, 0)
    middle = act_ref[...].reshape(512, act_ref.shape[2])
    edge_message((near_out, away_out), source, (base, 20 - base), (at, 28 - at), near_ref, away_ref, middle)


def input_message(flags_ref, near_ref, away_ref, cot_ref, slide_ref, near_out, away_out):
    chans = slide_ref.shape[2]
    tall = near_out.shape[0] - 48
    edge = near_ref.shape[0] - 64

    def source(at, base, row):
        if base is None:
            r = row - 1
            return jnp.where(jnp.logical_and(r >= 0, r < 32), r * 64 + at * 63, -1)
        return jnp.where(row == base, at * 63, -1)

    coarse_message(
        flags_ref, near_ref.at[:edge], away_ref.at[:edge], cot_ref, near_out.at[:tall], away_out.at[:tall]
    )
    base = jnp.where(flags_ref[0] == 0, 33, 0)
    at = jnp.where(flags_ref[1] == 0, 1, 0)
    middle = slide_ref[...].reshape(2048, chans)
    for out in (near_out, away_out):
        out[tall:, :] = jnp.zeros((48, out.shape[1]), BF)
    edge_message(
        (near_out.at[tall:, :chans], away_out.at[tall:, :chans]), source, (base, 33 - base), (at, 1 - at),
        near_ref.at[edge:, :chans], away_ref.at[edge:, :chans], middle,
    )


def fine_message(flags_ref, near_ref, away_ref, ddepth_ref, near_out, away_out):
    def source(at, base, row):
        if base is None:
            r = row - 1
            inside = jnp.logical_and(r >= 0, r < 32)
            return jnp.where(inside, ((r % 2) * 32 + r // 2) * 32 + at * 543, -1)
        return jnp.where(row == base, at * 63, -1)

    base = jnp.where(flags_ref[0] == 0, 33, 0)
    at = jnp.where(flags_ref[1] == 0, 1, 0)
    middle = ddepth_ref[...].reshape(2048, ddepth_ref.shape[3])
    edge_message((near_out, away_out), source, (base, 33 - base), (at, 1 - at), near_ref, away_ref, middle)


def side_rows(flags_ref, near_ref, away_ref, rows, width):
    def source(base, row):
        r, place = row // 16, row % 16 - base
        inside = jnp.logical_and(place >= 0, place < width)
        return jnp.where(inside, place * rows + r, -1)

    base = jnp.where(flags_ref[1] == 0, width, 0)
    total = 0.0
    for block, at in ((near_ref[...], base), (away_ref[...], width - base)):
        pick = picker(16 * rows, block.shape[0], functools.partial(source, at))
        total = total + dot(pick, block)
    return total.astype(BF).reshape(rows, 16, near_ref.shape[1])


def coarse_forward(
    flags_ref, act_ref, near_ref, away_ref, nside_ref, aside_ref, taps_ref, mix_ref, reduced_ref, cot_ref, deltac_ref,
    gred_ref, gmixf_ref, gtapsf_ref,
    section_out, mine_out, other_out, shifted, sums, depth, rows, sides_of, packed,
):
    wide = mix_ref.shape[0]
    for parity in range(2):

        @pl.when(flags_ref[0] == parity)
        def _():
            low, high = (near_ref, away_ref) if parity else (away_ref, near_ref)
            rows[0:4] = low[...].reshape(4, 32, wide)
            rows[20:24] = high[...].reshape(4, 32, wide)

    rows[4:20] = act_ref[...]
    sides_of[...] = side_rows(flags_ref, nside_ref, aside_ref, 24, 4)
    coarse_rows(lambda r: rows[r], lambda r: sides_of[r], shifted)
    sums[...] = jnp.zeros_like(sums)

    def conv(i, carry):
        total = None
        grad = deltac_ref[i].astype(F4)
        for a in range(5):
            for b in range(5):
                at = 5 * a + b
                window = shifted[b, i + 2 * a]
                term = taps_ref[a, b : b + 1, :] * window
                total = term if total is None else total + term
                sums[at] += jnp.sum((grad * window).reshape(4, 8, wide), axis=0)
        depth[i] = total.astype(BF)
        return carry

    lax.fori_loop(0, 16, conv, 0, unroll=2)
    flat = depth[...].reshape(512, wide)
    section_out[...] = (reduced_ref[...].reshape(512, wide).astype(F4) + dot(flat, mix_ref[...])).astype(BF).reshape(16, 32, wide)
    fine = jnp.concatenate([gmixf_ref[...], gtapsf_ref[...]], axis=0).astype(BF)
    spread = picker(wide, LANES, lambda row: row)
    for j in range(3):
        rows_of = slice(j * FINE, (j + 1) * FINE)
        both = dot(gred_ref[rows_of, :], spread) + dot(fine, piece(j, fine.shape[1], wide))
        packed[rows_of, :] = both.astype(BF)
    packed[3 * FINE :, :] = jnp.zeros((TOTAL - 3 * FINE, LANES), BF)
    packed[3 * FINE : MIXC, 0:wide] = gred_ref[3 * FINE :, :]
    packed[MIXC:TAPC, 0:wide] = dot_tn(flat, cot_ref[...].reshape(512, wide)).astype(BF)
    taps = jnp.concatenate([jnp.sum(sums[...], axis=1), jnp.zeros((7, wide), F4)], axis=0)
    packed[TAPC:TOTAL, 0:wide] = taps.astype(BF)
    core = flags_ref[2]
    half = TOTAL // 2
    mine_out[...] = packed[pl.ds(pl.multiple_of(core * half, half), half), :]
    other_out[...] = packed[pl.ds(pl.multiple_of((1 - core) * half, half), half), :]


def unpack(
    flags_ref, near_ref, far_ref, tapsf_out, mixf_out, red_out, tapsc_out, mixc_out, packed, *, fine, coarse
):
    core = flags_ref[2]
    half = TOTAL // 2
    packed[pl.ds(pl.multiple_of(core * half, half), half), :] = near_ref[...]
    packed[pl.ds(pl.multiple_of((1 - core) * half, half), half), :] = far_ref[...]
    chans = mixf_out.shape[0]
    wide = mixc_out.shape[0]
    red_out[...] = (packed[0:MIXC, 0:wide].astype(F4) * coarse).T
    mixc_out[...] = packed[MIXC:TAPC, 0:wide].astype(F4) * coarse
    total = 0.0
    for j in range(3):
        total = total + dot_nt(packed[j * FINE : (j + 1) * FINE, :], piece(j, chans, wide))
    mixf_out[...] = total[:chans] * fine
    taps = total[chans:] * fine
    for a in range(3):
        tapsf_out[a] = taps[3 * a : 3 * a + 3]
    taps = packed[TAPC:TOTAL, 0:wide].astype(F4) * coarse
    for a in range(5):
        tapsc_out[a] = taps[5 * a : 5 * a + 5]


def fine_backward(
    flags_ref, ddepth_ref, near_ref, away_ref, nside_ref, aside_ref, taps_ref, dfine_ref, slide_ref, out_ref,
    shifted, lr_ref, ends,
):
    chans = taps_ref.shape[2]
    pick = picker(64, 80, phase_source)
    weave = picker(64, 64, weave_source)

    def put(r, even, odd):
        got = dot(pick, jnp.concatenate([even, odd, lr_ref[r]], axis=0))
        shifted[0, r] = even.astype(F4)
        shifted[1, r] = odd.astype(F4)
        shifted[2, r] = got[:32]
        shifted[3, r] = got[32:]

    lr_ref[...] = side_rows(flags_ref, nside_ref, aside_ref, 48, 1)
    for parity in range(2):

        @pl.when(flags_ref[0] == parity)
        def _():
            low, high = (near_ref, away_ref) if parity else (away_ref, near_ref)
            ends[0] = low[...]
            ends[1] = high[...]

    put(0, ends[0, :32], ends[0, 32:])
    put(33, ends[1, :32], ends[1, 32:])

    def fill(i, carry):
        for p in range(2):
            put(2 * i + p + 1, ddepth_ref[2 * p, i], ddepth_ref[2 * p + 1, i])
        return carry

    lax.fori_loop(0, 16, fill, 0, unroll=True)

    def conv(i, carry):
        found = {}

        def put_one(k, value):
            slide = slide_ref[k, i].astype(F4)
            kept = jnp.where(slide > 0, value, 0.0)
            found[k] = (dfine_ref[k, i].astype(F4) + kept).astype(BF)

        fine_conv(i, shifted, taps_ref, True, put_one)
        for p in range(2):
            both = jnp.concatenate([found[2 * p], found[2 * p + 1]], axis=0)
            out_ref[2 * i + p] = dot(weave, both).astype(BF)
        return carry

    lax.fori_loop(0, 16, conv, 0, unroll=2)


def call(body, outs, scratch, flops, *operands):
    def spec(kind):
        return pl.BlockSpec(memory_space=pltpu.SMEM if kind == jnp.int32 else pltpu.VMEM)

    return pl.pallas_call(
        body,
        out_shape=[jax.ShapeDtypeStruct(shape, kind) for shape, kind in outs],
        in_specs=[spec(operand.dtype) for operand in operands],
        out_specs=[spec(kind) for _, kind in outs],
        scratch_shapes=[pltpu.VMEM(shape, kind) for shape, kind in scratch],
        compiler_params=pltpu.CompilerParams(vmem_limit_bytes=LIMIT),
        cost_estimate=pl.CostEstimate(flops=flops, bytes_accessed=8_000_000, transcendentals=0),
    )(*operands)


def trade(first, last, axes):
    even = lax.axis_index(axes) % 2 == 0
    return send(jnp.where(even, last, first), jnp.where(even, first, last), axes)


def send(near, away, axes):
    count = lax.axis_size(axes)
    far = [(i, i + 1) for i in range(1, count - 1, 2)]
    far = far + [(j, i) for i, j in far]
    return (
        lax.ppermute(near, axes, [(i, i ^ 1) for i in range(count)]),
        lax.ppermute(away, axes, far),
    )


def coarse_edges(coarse):
    height, breadth, wide = coarse.shape
    return coarse[:4].reshape(4 * breadth, wide), coarse[-4:].reshape(4 * breadth, wide)


def coarse_sides(left, right):
    wide = left.shape[1]

    def spread(block):
        return block.reshape(4, -1, wide).transpose(1, 0, 2)

    return sides(spread(left), spread(right))


def fine_sides(left, right):
    return sides(left[:, None], right[:, None])


def stack_rows(coarse, fine):
    widened = jnp.pad(fine, ((0, 0), (0, coarse.shape[1] - fine.shape[1])))
    return jnp.concatenate([coarse, widened], axis=0)


def input_halos(flags, coarse, fine):
    height, breadth, wide = coarse.shape
    chans = fine.shape[-1]
    first, last = coarse_edges(coarse)
    split = 4 * breadth
    near, away = trade(stack_rows(first, fine[0]), stack_rows(last, fine[-1]), ROWS)
    tall = 4 * (height + 8)
    shape = (tall + 48, wide)
    message = call(
        input_message, [(shape, BF), (shape, BF)], [], 10_000_000, flags, near, away, coarse, fine
    )
    even = lax.axis_index(ROWS) % 2 == 0
    low, high = jnp.where(even, away, near), jnp.where(even, near, away)
    top, bottom = low[:split].reshape(4, breadth, wide), high[:split].reshape(4, breadth, wide)
    near, away = send(*message, COLS)
    even = lax.axis_index(COLS) % 2 == 0
    left, right = jnp.where(even, away, near), jnp.where(even, near, away)
    side_coarse = coarse_sides(left[:tall], right[:tall])
    side_fine = fine_sides(left[tall : tall + 34, :chans], right[tall : tall + 34, :chans])
    return top, bottom, side_coarse, low[split:, :chans], high[split:, :chans], side_fine


def hold(value, *others):
    return lax.optimization_barrier((value, *others))[0]


def reduce_terms(mine, other, rows_step, columns_step, last_step):
    total, lanes = mine.shape
    core = lax.axis_index("core")
    plane = lax.axis_size(PLANE)
    depth = lax.axis_size("z")
    across = [(0, 1), (1, 0)]
    mine = mine + lax.ppermute(other, "core", across)
    chunk = total // plane
    mine = mine.reshape(plane, chunk, lanes)
    edges = rows_step(mine)
    got = lax.all_to_all(mine, PLANE, 0, 0, tiled=True)
    mine = jnp.sum(got.astype(F4), axis=0).astype(BF)
    mine, edges = lax.optimization_barrier((mine, edges))
    edges = columns_step(edges)
    got = lax.all_to_all(jnp.broadcast_to(mine, (depth, chunk, lanes)), "z", 0, 0, tiled=True)
    mine = jnp.sum(got.astype(F4), axis=0).astype(BF)
    mine, edges = lax.optimization_barrier((mine, edges))
    extra = last_step(edges)
    got = lax.all_to_all(jnp.broadcast_to(mine, (plane, chunk, lanes)), PLANE, 0, 0, tiled=True)
    got, extra = lax.optimization_barrier((got.reshape(total, lanes), extra))
    return got, lax.ppermute(got, "core", across), extra


def sides(left, right):
    both = jnp.concatenate([left, right], axis=1)
    return jnp.pad(both, ((0, 0), (0, 16 - both.shape[1]), (0, 0)))


def shards(slide_pixels, taps_fine, mix_fine, reduce_weight, taps_coarse, mix_coarse, cotangent):
    height, breadth, chans = slide_pixels.shape
    wide = cotangent.shape[2]
    devices_all = lax.axis_size(ROWS) * lax.axis_size(COLS)
    scale_fine = float(height * breadth * devices_all) ** (-0.5)
    scale_coarse = float(height * breadth // 4 * devices_all) ** (-0.5)
    flags = jnp.stack(
        [lax.axis_index(ROWS) % 2, lax.axis_index(COLS) % 2, lax.axis_index("core")]
    ).astype(jnp.int32)
    ctop, cbottom, clr, top, bottom, lr = input_halos(flags, cotangent, slide_pixels)
    top, bottom = top[None], bottom[None]

    slide, depth, pre, reduced, act = call(
        fine_forward,
        [
            ((4, 16, 32, chans), BF),
            ((4, 16, 32, chans), BF),
            ((4, 512, chans), BF),
            ((512, wide), BF),
            ((16, 32, wide), BF),
        ],
        [((4, 34, 32, chans), F4), ((512, wide), F4)],
        4_000_000_000,
        slide_pixels, top, bottom, lr, taps_fine, mix_fine, reduce_weight,
    )
    reduced = reduced.reshape(16, 32, wide)

    delta_coarse, delta_reduced = call(
        coarse_backward,
        [((16, 32, wide), BF), ((16, 32, wide), BF)],
        [((24, 32, wide), BF), ((24, 16, wide), BF), ((5, 24, 32, wide), F4)],
        8_000_000_000,
        cotangent, jnp.concatenate([ctop, cbottom], axis=0), clr, mix_coarse, taps_coarse, reduced,
    )
    arows = trade(*coarse_edges(act), ROWS)
    arows, delta_reduced = lax.optimization_barrier((arows, delta_reduced))
    tall = 4 * (height // 2 + 8)
    message = call(
        coarse_message, [((tall, wide), BF), ((tall, wide), BF)], [], 10_000_000, flags, *arows, act
    )
    acolumns = send(*message, COLS)
    dfine, ddepth, term_reduce, term_mix_fine, term_taps_fine = call(
        fine_terms,
        [
            ((4, 16, 32, chans), BF),
            ((4, 16, 32, chans), BF),
            ((4 * chans, wide), BF),
            ((chans, chans), F4),
            ((16, chans), F4),
        ],
        [((4, 34, 32, chans), F4)],
        8_000_000_000,
        delta_reduced.reshape(512, wide), pre, depth.reshape(4, 512, chans), reduce_weight, mix_fine,
        slide_pixels, top, bottom, lr,
    )
    acolumns, ddepth = lax.optimization_barrier((acolumns, ddepth))
    section_out, mine, other = call(
        coarse_forward,
        [((16, 32, wide), BF), ((TOTAL // 2, LANES), BF), ((TOTAL // 2, LANES), BF)],
        [
            ((5, 24, 32, wide), F4),
            ((25, 8, wide), F4),
            ((16, 32, wide), BF),
            ((24, 32, wide), BF),
            ((24, 16, wide), BF),
            ((TOTAL, LANES), BF),
        ],
        4_000_000_000,
        flags, act, *arows, *acolumns, taps_coarse, mix_coarse, reduced, cotangent, delta_coarse,
        term_reduce, term_mix_fine, term_taps_fine,
    )
    def rows_step(after):
        edges = ddepth[:2, 0].reshape(breadth, chans), ddepth[2:, 15].reshape(breadth, chans)
        return trade(*hold(edges, after), ROWS)

    def columns_step(rows):
        message = call(
            fine_message, [((48, chans), BF), ((48, chans), BF)], [], 10_000_000, flags, *rows, ddepth
        )
        return *rows, *send(*message, COLS)

    def last_step(edges):
        return call(
            fine_backward,
            [((height, breadth, chans), BF)],
            [((4, 34, 32, chans), F4), ((48, 16, chans), BF), ((2, 64, chans), BF)],
            2_000_000_000,
            flags, ddepth, *edges, taps_fine, dfine, slide,
        )[0]

    near, far, pixel_grad = reduce_terms(mine, other, rows_step, columns_step, last_step)
    grads = call(
        functools.partial(unpack, fine=scale_fine, coarse=scale_coarse),
        [
            ((3, 3, chans), F4),
            ((chans, chans), F4),
            ((wide, 4 * chans), F4),
            ((5, 5, wide), F4),
            ((wide, wide), F4),
        ],
        [((TOTAL, LANES), BF)],
        1_000_000,
        flags, near, far,
    )
    tapsf, mixf, red, tapsc, mixc = grads
    return (section_out, pixel_grad, tapsf, mixf, red.T, tapsc, mixc)


def solution(mesh):
    fine = Mesh(mesh.devices.reshape(2, 2, 4, 2, 8), ("yl", "core", "x", "yh", "z"))
    tiles = P(ROWS, COLS, None)
    return jax.shard_map(
        shards,
        mesh=fine,
        in_specs=(tiles, P(), P(), P(), P(), P(), tiles),
        out_specs=(tiles, tiles, P(), P(), P(), P(), P()),
        check_vma=False,
    )
```

```python
import functools

import jax
import jax.numpy as jnp
from jax import lax
from jax.experimental import pallas as pl
from jax.experimental.pallas import tpu as pltpu
from jax.sharding import Mesh, PartitionSpec as P

ROWS = ("yl", "core")
COLS = ("x", "yh", "z")
PLANE = ("yl", "x", "yh")
BF = jnp.bfloat16
F4 = jnp.float32
LIMIT = 28 * 1024 * 1024
MIXC, TAPC, TOTAL, FINE = 832, 1248, 1280, 224
LANES = 512
SOURCE = ((2, 0, 1), (0, 1, 3))


def dot(left, right):
    return jnp.dot(left, right, preferred_element_type=F4)


def dot_nt(left, right):
    return lax.dot_general(left, right, (((1,), (1,)), ((), ())), preferred_element_type=F4)


def dot_tn(left, right):
    return lax.dot_general(left, right, (((0,), (0,)), ((), ())), preferred_element_type=F4)


def picker(rows, columns, source):
    row = lax.broadcasted_iota(jnp.int32, (rows, columns), 0)
    column = lax.broadcasted_iota(jnp.int32, (rows, columns), 1)
    return jnp.where(column == source(row), 1.0, 0.0).astype(BF)


def fine_source(row):
    kind, m = row // 32, row % 32
    even, odd = 2 * m, 2 * m + 1
    before = jnp.where(m == 0, 64, 2 * m - 1)
    after = jnp.where(m == 31, 65, 2 * m + 2)
    return jnp.where(kind == 0, even, jnp.where(kind == 1, odd, jnp.where(kind == 2, before, after)))


def phase_source(row):
    kind, m = row // 32, row % 32
    before = jnp.where(m == 0, 64, 32 + m - 1)
    after = jnp.where(m == 31, 65, m + 1)
    return jnp.where(kind == 0, before, after)


def weave_source(row):
    return jnp.where(row % 2 == 0, row // 2, 32 + row // 2)


def coarse_source(row):
    shift, m = row // 32, row % 32
    at = m + 2 * shift - 4
    return jnp.where(at < 0, 36 + at, jnp.where(at > 31, 4 + at, at))


def sigmoid(value):
    return 0.5 * jnp.tanh(0.5 * value) + 0.5


def fine_rows(slide_ref, top_ref, bottom_ref, lr_ref, shifted, keep=None):
    pick = picker(128, 80, fine_source)

    def put(r, row):
        got = dot(pick, jnp.concatenate([row, lr_ref[r]], axis=0))
        shifted[:, r] = jnp.maximum(got, 0.0).reshape(4, 32, got.shape[1])
        return got

    put(0, top_ref[0])
    put(33, bottom_ref[0])

    def step(i, carry):
        for p in range(2):
            got = put(2 * i + p + 1, slide_ref[2 * i + p])
            if keep is not None:
                keep[2 * p, i] = got[:32].astype(BF)
                keep[2 * p + 1, i] = got[32:64].astype(BF)
        return carry

    lax.fori_loop(0, 16, step, 0, unroll=True)


def fine_conv(i, shifted, taps_ref, flip, put):
    for p in range(2):
        for q in range(2):
            total = None
            for a in range(3):
                for b in range(3):
                    u, v = (2 - a, 2 - b) if flip else (a, b)
                    term = taps_ref[u, v : v + 1, :] * shifted[SOURCE[q][b], 2 * i + p + a]
                    total = term if total is None else total + term
            put(2 * p + q, total)


def fine_forward(
    slide_ref, top_ref, bottom_ref, lr_ref, taps_ref, mix_ref, weight_ref,
    slide_out, depth_out, pre_out, reduced_out, act_out, shifted, total,
):
    fine_rows(slide_ref, top_ref, bottom_ref, lr_ref, shifted, slide_out)

    def conv(i, carry):
        def put(k, value):
            depth_out[k, i] = value.astype(BF)

        fine_conv(i, shifted, taps_ref, False, put)
        return carry

    lax.fori_loop(0, 16, conv, 0, unroll=4)
    chans = mix_ref.shape[0]
    wide = weight_ref.shape[1]
    for k in range(4):
        mixed = dot(depth_out[k].reshape(512, chans), mix_ref[...])
        pre = (slide_out[k].reshape(512, chans).astype(F4) + mixed).astype(BF)
        pre_out[k] = pre
        value = pre.astype(F4)
        unshuffled = (value * sigmoid(value)).astype(BF)
        part = dot(unshuffled, weight_ref[k * chans : (k + 1) * chans, :])
        if k == 0:
            total[...] = part
        else:
            total[...] += part
    reduced = total[...].astype(BF)
    reduced_out[...] = reduced
    value = reduced.astype(F4)
    act_out[...] = (value * sigmoid(value)).astype(BF).reshape(16, 32, wide)


def coarse_rows(row_of, lr_of, shifted):
    pick = picker(160, 48, coarse_source)

    def step(r, carry):
        got = dot(pick, jnp.concatenate([row_of(r), lr_of(r)], axis=0))
        shifted[:, r] = got.reshape(5, 32, got.shape[1])
        return carry

    lax.fori_loop(0, 24, step, 0, unroll=True)


def coarse_backward(
    cot_ref, tb_ref, lr_ref, mixc_ref, tapsc_ref, reduced_ref, deltac_out, delta_red, delta, delta_lr, shiftc
):
    wide = mixc_ref.shape[0]
    mixc = mixc_ref[...]
    inner = dot_nt(cot_ref[...].reshape(512, wide), mixc).astype(BF).reshape(16, 32, wide)
    delta[4:20] = inner
    deltac_out[...] = inner
    edge = dot_nt(tb_ref[...].reshape(256, wide), mixc).astype(BF).reshape(8, 32, wide)
    delta[0:4] = edge[:4]
    delta[20:24] = edge[4:]
    delta_lr[...] = dot_nt(lr_ref[...].reshape(384, wide), mixc).astype(BF).reshape(24, 16, wide)
    coarse_rows(lambda r: delta[r], lambda r: delta_lr[r], shiftc)

    def conv(i, carry):
        total = None
        for a in range(5):
            for b in range(5):
                term = tapsc_ref[4 - a, 4 - b : 5 - b, :] * shiftc[b, i + 2 * a]
                total = term if total is None else total + term
        back = total.astype(BF).astype(F4)
        value = reduced_ref[i].astype(F4)
        s = sigmoid(value)
        slope = s * (1.0 + value * (1.0 - s))
        delta_red[i] = (cot_ref[i].astype(F4) + back * slope).astype(BF)
        return carry

    lax.fori_loop(0, 16, conv, 0, unroll=4)


def fine_terms(
    red_ref, pre_ref, depth_ref, weight_ref, mix_ref, slide_ref, top_ref, bottom_ref, lrf_ref,
    dfine_out, ddepth_out, gred_out, gmix_out, gtaps_out, shifted,
):
    chans = mix_ref.shape[0]
    fine_rows(slide_ref, top_ref, bottom_ref, lrf_ref, shifted)
    red = red_ref[...]
    for k in range(4):
        value = pre_ref[k].astype(F4)
        s = sigmoid(value)
        unshuffled = (value * s).astype(BF)
        gred_out[k * chans : (k + 1) * chans, :] = dot_tn(unshuffled, red).astype(BF)
        spread = dot_nt(red, weight_ref[k * chans : (k + 1) * chans, :])
        dfine = (spread * (s * (1.0 + value * (1.0 - s)))).astype(BF)
        dfine_out[k] = dfine.reshape(16, 32, chans)
        part = dot_tn(depth_ref[k], dfine)
        if k == 0:
            gmix_out[...] = part
        else:
            gmix_out[...] += part
        ddepth_out[k] = dot_nt(dfine, mix_ref[...]).astype(BF).reshape(16, 32, chans)

    def taps(i, sums):
        for p in range(2):
            for q in range(2):
                grad = ddepth_out[2 * p + q, i].astype(F4)
                fresh = []
                for a in range(3):
                    for b in range(3):
                        term = grad * shifted[SOURCE[q][b], 2 * i + p + a]
                        fresh.append(sums[3 * a + b] + jnp.sum(term.reshape(4, 8, chans), axis=0))
                sums = tuple(fresh)
        return sums

    sums = lax.fori_loop(0, 16, taps, tuple(jnp.zeros((8, chans), F4) for _ in range(9)), unroll=2)
    gtaps_out[...] = jnp.zeros_like(gtaps_out)
    for at in range(9):
        gtaps_out[at : at + 1, :] = jnp.sum(sums[at], axis=0, keepdims=True)


def piece(j, chans, wide):
    room = LANES - wide
    return picker(
        chans, 128, lambda row: jnp.where(row // room == j, 128 - room + row % room, -1)
    )


def edge_message(outs, source, bases, ats, near_ref, away_ref, middle):
    for out, at in zip(outs, ats):
        total = 0.0
        for block, base in ((near_ref[...], bases[0]), (away_ref[...], bases[1]), (middle, None)):
            pick = picker(out.shape[0], block.shape[0], functools.partial(source, at, base))
            total = total + dot(pick, block)
        out[...] = total.astype(BF)


def coarse_message(flags_ref, near_ref, away_ref, act_ref, near_out, away_out):
    def source(at, base, row):
        column, r = row // 24, row % 24
        if base is None:
            inside = jnp.logical_and(r >= 4, r < 20)
            return jnp.where(inside, (r - 4) * 32 + at + column, -1)
        inside = jnp.logical_and(r >= base, r < base + 4)
        return jnp.where(inside, (r - base) * 32 + at + column, -1)

    base = jnp.where(flags_ref[0] == 0, 20, 0)
    at = jnp.where(flags_ref[1] == 0, 28, 0)
    middle = act_ref[...].reshape(512, act_ref.shape[2])
    edge_message((near_out, away_out), source, (base, 20 - base), (at, 28 - at), near_ref, away_ref, middle)


def input_message(flags_ref, near_ref, away_ref, cot_ref, slide_ref, near_out, away_out):
    chans = slide_ref.shape[2]
    tall = near_out.shape[0] - 48
    edge = near_ref.shape[0] - 64

    def source(at, base, row):
        if base is None:
            r = row - 1
            return jnp.where(jnp.logical_and(r >= 0, r < 32), r * 64 + at * 63, -1)
        return jnp.where(row == base, at * 63, -1)

    coarse_message(
        flags_ref, near_ref.at[:edge], away_ref.at[:edge], cot_ref, near_out.at[:tall], away_out.at[:tall]
    )
    base = jnp.where(flags_ref[0] == 0, 33, 0)
    at = jnp.where(flags_ref[1] == 0, 1, 0)
    middle = slide_ref[...].reshape(2048, chans)
    for out in (near_out, away_out):
        out[tall:, :] = jnp.zeros((48, out.shape[1]), BF)
    edge_message(
        (near_out.at[tall:, :chans], away_out.at[tall:, :chans]), source, (base, 33 - base), (at, 1 - at),
        near_ref.at[edge:, :chans], away_ref.at[edge:, :chans], middle,
    )


def fine_message(flags_ref, near_ref, away_ref, ddepth_ref, near_out, away_out):
    def source(at, base, row):
        if base is None:
            r = row - 1
            inside = jnp.logical_and(r >= 0, r < 32)
            return jnp.where(inside, ((r % 2) * 32 + r // 2) * 32 + at * 543, -1)
        return jnp.where(row == base, at * 63, -1)

    base = jnp.where(flags_ref[0] == 0, 33, 0)
    at = jnp.where(flags_ref[1] == 0, 1, 0)
    middle = ddepth_ref[...].reshape(2048, ddepth_ref.shape[3])
    edge_message((near_out, away_out), source, (base, 33 - base), (at, 1 - at), near_ref, away_ref, middle)


def side_rows(flags_ref, near_ref, away_ref, rows, width):
    def source(base, row):
        r, place = row // 16, row % 16 - base
        inside = jnp.logical_and(place >= 0, place < width)
        return jnp.where(inside, place * rows + r, -1)

    base = jnp.where(flags_ref[1] == 0, width, 0)
    total = 0.0
    for block, at in ((near_ref[...], base), (away_ref[...], width - base)):
        pick = picker(16 * rows, block.shape[0], functools.partial(source, at))
        total = total + dot(pick, block)
    return total.astype(BF).reshape(rows, 16, near_ref.shape[1])


def coarse_forward(
    flags_ref, act_ref, near_ref, away_ref, nside_ref, aside_ref, taps_ref, mix_ref, reduced_ref, cot_ref, deltac_ref,
    gred_ref, gmixf_ref, gtapsf_ref,
    section_out, mine_out, other_out, shifted, sums, depth, rows, sides_of, packed,
):
    wide = mix_ref.shape[0]
    for parity in range(2):

        @pl.when(flags_ref[0] == parity)
        def _():
            low, high = (near_ref, away_ref) if parity else (away_ref, near_ref)
            rows[0:4] = low[...].reshape(4, 32, wide)
            rows[20:24] = high[...].reshape(4, 32, wide)

    rows[4:20] = act_ref[...]
    sides_of[...] = side_rows(flags_ref, nside_ref, aside_ref, 24, 4)
    coarse_rows(lambda r: rows[r], lambda r: sides_of[r], shifted)
    sums[...] = jnp.zeros_like(sums)

    def conv(i, carry):
        total = None
        grad = deltac_ref[i].astype(F4)
        for a in range(5):
            for b in range(5):
                at = 5 * a + b
                window = shifted[b, i + 2 * a]
                term = taps_ref[a, b : b + 1, :] * window
                total = term if total is None else total + term
                sums[at] += jnp.sum((grad * window).reshape(4, 8, wide), axis=0)
        depth[i] = total.astype(BF)
        return carry

    lax.fori_loop(0, 16, conv, 0, unroll=4)
    flat = depth[...].reshape(512, wide)
    section_out[...] = (reduced_ref[...].reshape(512, wide).astype(F4) + dot(flat, mix_ref[...])).astype(BF).reshape(16, 32, wide)
    fine = jnp.concatenate([gmixf_ref[...], gtapsf_ref[...]], axis=0).astype(BF)
    full = LANES - 128
    spread = picker(wide - full, 128, lambda row: row)
    for j in range(3):
        rows_of = slice(j * FINE, (j + 1) * FINE)
        both = dot(gred_ref[rows_of, full:], spread) + dot(fine, piece(j, fine.shape[1], wide))
        packed[rows_of, :full] = gred_ref[rows_of, :full]
        packed[rows_of, full:] = both.astype(BF)
    packed[3 * FINE :, :] = jnp.zeros((TOTAL - 3 * FINE, LANES), BF)
    packed[3 * FINE : MIXC, 0:wide] = gred_ref[3 * FINE :, :]
    packed[MIXC:TAPC, 0:wide] = dot_tn(flat, cot_ref[...].reshape(512, wide)).astype(BF)
    taps = jnp.concatenate([jnp.sum(sums[...], axis=1), jnp.zeros((7, wide), F4)], axis=0)
    packed[TAPC:TOTAL, 0:wide] = taps.astype(BF)
    core = flags_ref[2]
    half = TOTAL // 2
    mine_out[...] = packed[pl.ds(pl.multiple_of(core * half, half), half), :]
    other_out[...] = packed[pl.ds(pl.multiple_of((1 - core) * half, half), half), :]


def unpack(
    flags_ref, near_ref, far_ref, tapsf_out, mixf_out, red_out, tapsc_out, mixc_out, packed, *, fine, coarse
):
    core = flags_ref[2]
    half = TOTAL // 2
    packed[pl.ds(pl.multiple_of(core * half, half), half), :] = near_ref[...]
    packed[pl.ds(pl.multiple_of((1 - core) * half, half), half), :] = far_ref[...]
    chans = mixf_out.shape[0]
    wide = mixc_out.shape[0]
    red_out[...] = (packed[0:MIXC, 0:wide].astype(F4) * coarse).T
    mixc_out[...] = packed[MIXC:TAPC, 0:wide].astype(F4) * coarse
    total = 0.0
    for j in range(3):
        total = total + dot_nt(packed[j * FINE : (j + 1) * FINE, LANES - 128 :], piece(j, chans, wide))
    mixf_out[...] = total[:chans] * fine
    taps = total[chans:] * fine
    for a in range(3):
        tapsf_out[a] = taps[3 * a : 3 * a + 3]
    taps = packed[TAPC:TOTAL, 0:wide].astype(F4) * coarse
    for a in range(5):
        tapsc_out[a] = taps[5 * a : 5 * a + 5]


def fine_backward(
    flags_ref, ddepth_ref, near_ref, away_ref, nside_ref, aside_ref, taps_ref, dfine_ref, slide_ref, out_ref,
    shifted, lr_ref, ends,
):
    chans = taps_ref.shape[2]
    pick = picker(64, 80, phase_source)
    weave = picker(64, 64, weave_source)

    def put(r, even, odd):
        got = dot(pick, jnp.concatenate([even, odd, lr_ref[r]], axis=0))
        shifted[0, r] = even.astype(F4)
        shifted[1, r] = odd.astype(F4)
        shifted[2, r] = got[:32]
        shifted[3, r] = got[32:]

    lr_ref[...] = side_rows(flags_ref, nside_ref, aside_ref, 48, 1)
    for parity in range(2):

        @pl.when(flags_ref[0] == parity)
        def _():
            low, high = (near_ref, away_ref) if parity else (away_ref, near_ref)
            ends[0] = low[...]
            ends[1] = high[...]

    put(0, ends[0, :32], ends[0, 32:])
    put(33, ends[1, :32], ends[1, 32:])

    def fill(i, carry):
        for p in range(2):
            put(2 * i + p + 1, ddepth_ref[2 * p, i], ddepth_ref[2 * p + 1, i])
        return carry

    lax.fori_loop(0, 16, fill, 0, unroll=True)

    def conv(i, carry):
        found = {}

        def put_one(k, value):
            slide = slide_ref[k, i].astype(F4)
            kept = jnp.where(slide > 0, value, 0.0)
            found[k] = (dfine_ref[k, i].astype(F4) + kept).astype(BF)

        fine_conv(i, shifted, taps_ref, True, put_one)
        for p in range(2):
            both = jnp.concatenate([found[2 * p], found[2 * p + 1]], axis=0)
            out_ref[2 * i + p] = dot(weave, both).astype(BF)
        return carry

    lax.fori_loop(0, 16, conv, 0, unroll=4)


def call(body, outs, scratch, flops, *operands):
    def spec(kind):
        return pl.BlockSpec(memory_space=pltpu.SMEM if kind == jnp.int32 else pltpu.VMEM)

    return pl.pallas_call(
        body,
        out_shape=[jax.ShapeDtypeStruct(shape, kind) for shape, kind in outs],
        in_specs=[spec(operand.dtype) for operand in operands],
        out_specs=[spec(kind) for _, kind in outs],
        scratch_shapes=[pltpu.VMEM(shape, kind) for shape, kind in scratch],
        compiler_params=pltpu.CompilerParams(vmem_limit_bytes=LIMIT),
        cost_estimate=pl.CostEstimate(flops=flops, bytes_accessed=8_000_000, transcendentals=0),
    )(*operands)


def trade(first, last, axes):
    even = lax.axis_index(axes) % 2 == 0
    return send(jnp.where(even, last, first), jnp.where(even, first, last), axes)


def send(near, away, axes):
    count = lax.axis_size(axes)
    far = [(i, i + 1) for i in range(1, count - 1, 2)]
    far = far + [(j, i) for i, j in far]
    return (
        lax.ppermute(near, axes, [(i, i ^ 1) for i in range(count)]),
        lax.ppermute(away, axes, far),
    )


def coarse_edges(coarse):
    height, breadth, wide = coarse.shape
    return coarse[:4].reshape(4 * breadth, wide), coarse[-4:].reshape(4 * breadth, wide)


def coarse_sides(left, right):
    wide = left.shape[1]

    def spread(block):
        return block.reshape(4, -1, wide).transpose(1, 0, 2)

    return sides(spread(left), spread(right))


def fine_sides(left, right):
    return sides(left[:, None], right[:, None])


def stack_rows(coarse, fine):
    widened = jnp.pad(fine, ((0, 0), (0, coarse.shape[1] - fine.shape[1])))
    return jnp.concatenate([coarse, widened], axis=0)


def input_halos(flags, coarse, fine):
    height, breadth, wide = coarse.shape
    chans = fine.shape[-1]
    first, last = coarse_edges(coarse)
    split = 4 * breadth
    near, away = trade(stack_rows(first, fine[0]), stack_rows(last, fine[-1]), ROWS)
    tall = 4 * (height + 8)
    shape = (tall + 48, wide)
    message = call(
        input_message, [(shape, BF), (shape, BF)], [], 10_000_000, flags, near, away, coarse, fine
    )
    even = lax.axis_index(ROWS) % 2 == 0
    low, high = jnp.where(even, away, near), jnp.where(even, near, away)
    top, bottom = low[:split].reshape(4, breadth, wide), high[:split].reshape(4, breadth, wide)
    near, away = send(*message, COLS)
    even = lax.axis_index(COLS) % 2 == 0
    left, right = jnp.where(even, away, near), jnp.where(even, near, away)
    side_coarse = coarse_sides(left[:tall], right[:tall])
    side_fine = fine_sides(left[tall : tall + 34, :chans], right[tall : tall + 34, :chans])
    return top, bottom, side_coarse, low[split:, :chans], high[split:, :chans], side_fine


def hold(value, *others):
    return lax.optimization_barrier((value, *others))[0]


def reduce_terms(mine, other, rows_step, columns_step, last_step):
    total, lanes = mine.shape
    core = lax.axis_index("core")
    plane = lax.axis_size(PLANE)
    depth = lax.axis_size("z")
    across = [(0, 1), (1, 0)]
    mine = mine + lax.ppermute(other, "core", across)
    chunk = total // plane
    mine = mine.reshape(plane, chunk, lanes)
    edges = rows_step(mine)
    got = lax.all_to_all(mine, PLANE, 0, 0, tiled=True)
    mine = jnp.sum(got.astype(F4), axis=0).astype(BF)
    mine, edges = lax.optimization_barrier((mine, edges))
    edges = columns_step(edges)
    got = lax.all_to_all(jnp.broadcast_to(mine, (depth, chunk, lanes)), "z", 0, 0, tiled=True)
    mine = jnp.sum(got.astype(F4), axis=0).astype(BF)
    mine, edges = lax.optimization_barrier((mine, edges))
    extra = last_step(edges)
    got = lax.all_to_all(jnp.broadcast_to(mine, (plane, chunk, lanes)), PLANE, 0, 0, tiled=True)
    got, extra = lax.optimization_barrier((got.reshape(total, lanes), extra))
    return got, lax.ppermute(got, "core", across), extra


def sides(left, right):
    both = jnp.concatenate([left, right], axis=1)
    return jnp.pad(both, ((0, 0), (0, 16 - both.shape[1]), (0, 0)))


def shards(slide_pixels, taps_fine, mix_fine, reduce_weight, taps_coarse, mix_coarse, cotangent):
    height, breadth, chans = slide_pixels.shape
    wide = cotangent.shape[2]
    devices_all = lax.axis_size(ROWS) * lax.axis_size(COLS)
    scale_fine = float(height * breadth * devices_all) ** (-0.5)
    scale_coarse = float(height * breadth // 4 * devices_all) ** (-0.5)
    flags = jnp.stack(
        [lax.axis_index(ROWS) % 2, lax.axis_index(COLS) % 2, lax.axis_index("core")]
    ).astype(jnp.int32)
    ctop, cbottom, clr, top, bottom, lr = input_halos(flags, cotangent, slide_pixels)
    top, bottom = top[None], bottom[None]

    slide, depth, pre, reduced, act = call(
        fine_forward,
        [
            ((4, 16, 32, chans), BF),
            ((4, 16, 32, chans), BF),
            ((4, 512, chans), BF),
            ((512, wide), BF),
            ((16, 32, wide), BF),
        ],
        [((4, 34, 32, chans), F4), ((512, wide), F4)],
        4_000_000_000,
        slide_pixels, top, bottom, lr, taps_fine, mix_fine, reduce_weight,
    )
    reduced = reduced.reshape(16, 32, wide)

    delta_coarse, delta_reduced = call(
        coarse_backward,
        [((16, 32, wide), BF), ((16, 32, wide), BF)],
        [((24, 32, wide), BF), ((24, 16, wide), BF), ((5, 24, 32, wide), F4)],
        8_000_000_000,
        cotangent, jnp.concatenate([ctop, cbottom], axis=0), clr, mix_coarse, taps_coarse, reduced,
    )
    arows = trade(*coarse_edges(act), ROWS)
    arows, delta_reduced = lax.optimization_barrier((arows, delta_reduced))
    tall = 4 * (height // 2 + 8)
    message = call(
        coarse_message, [((tall, wide), BF), ((tall, wide), BF)], [], 10_000_000, flags, *arows, act
    )
    acolumns = send(*message, COLS)
    dfine, ddepth, term_reduce, term_mix_fine, term_taps_fine = call(
        fine_terms,
        [
            ((4, 16, 32, chans), BF),
            ((4, 16, 32, chans), BF),
            ((4 * chans, wide), BF),
            ((chans, chans), F4),
            ((16, chans), F4),
        ],
        [((4, 34, 32, chans), F4)],
        8_000_000_000,
        delta_reduced.reshape(512, wide), pre, depth.reshape(4, 512, chans), reduce_weight, mix_fine,
        slide_pixels, top, bottom, lr,
    )
    acolumns, ddepth = lax.optimization_barrier((acolumns, ddepth))
    section_out, mine, other = call(
        coarse_forward,
        [((16, 32, wide), BF), ((TOTAL // 2, LANES), BF), ((TOTAL // 2, LANES), BF)],
        [
            ((5, 24, 32, wide), F4),
            ((25, 8, wide), F4),
            ((16, 32, wide), BF),
            ((24, 32, wide), BF),
            ((24, 16, wide), BF),
            ((TOTAL, LANES), BF),
        ],
        4_000_000_000,
        flags, act, *arows, *acolumns, taps_coarse, mix_coarse, reduced, cotangent, delta_coarse,
        term_reduce, term_mix_fine, term_taps_fine,
    )
    def rows_step(after):
        edges = ddepth[:2, 0].reshape(breadth, chans), ddepth[2:, 15].reshape(breadth, chans)
        return trade(*hold(edges, after), ROWS)

    def columns_step(rows):
        message = call(
            fine_message, [((48, chans), BF), ((48, chans), BF)], [], 10_000_000, flags, *rows, ddepth
        )
        return *rows, *send(*message, COLS)

    def last_step(edges):
        return call(
            fine_backward,
            [((height, breadth, chans), BF)],
            [((4, 34, 32, chans), F4), ((48, 16, chans), BF), ((2, 64, chans), BF)],
            2_000_000_000,
            flags, ddepth, *edges, taps_fine, dfine, slide,
        )[0]

    near, far, pixel_grad = reduce_terms(mine, other, rows_step, columns_step, last_step)
    grads = call(
        functools.partial(unpack, fine=scale_fine, coarse=scale_coarse),
        [
            ((3, 3, chans), F4),
            ((chans, chans), F4),
            ((wide, 4 * chans), F4),
            ((5, 5, wide), F4),
            ((wide, wide), F4),
        ],
        [((TOTAL, LANES), BF)],
        1_000_000,
        flags, near, far,
    )
    tapsf, mixf, red, tapsc, mixc = grads
    return (section_out, pixel_grad, tapsf, mixf, red.T, tapsc, mixc)


def solution(mesh):
    fine = Mesh(mesh.devices.reshape(2, 2, 4, 2, 8), ("yl", "core", "x", "yh", "z"))
    tiles = P(ROWS, COLS, None)
    return jax.shard_map(
        shards,
        mesh=fine,
        in_specs=(tiles, P(), P(), P(), P(), P(), tiles),
        out_specs=(tiles, tiles, P(), P(), P(), P(), P()),
        check_vma=False,
    )
```
